128 devices in a mesh: rows: 8 (over y, z_lo), frames: 16 (over z_hi, x, core).
Axes of the slice: x: 4, y: 4, z: 4 (z_hi: 2, z_lo: 2; z = z_hi * 2 + z_lo), core: 2. Of those that a mesh axis runs over, the one named last changes fastest.
Arguments:
- latents: bfloat16 [16384, 128], P(('rows', 'frames')), may hold values from -6 to 6
- tile_slot: int32 [16384], P(('rows', 'frames')), may hold values from 0 to 16383, as said below
- w_in: bfloat16 [3, 3, 3, 16, 384], replicated, may hold values from -0.3125 to 0.3125
- b_in: float32 [384], replicated, may hold values from -3 to 3
- gain_in: float32 [384], replicated, may hold values from 0.1 to 1.9
- w_time: bfloat16 [3, 384, 768], replicated, may hold values from -0.1875 to 0.1875
- b_time: float32 [768], replicated, may hold values from -3 to 3
- w_lift: bfloat16 [3, 3, 384, 192], replicated, may hold values from -0.109375 to 0.109375
- b_lift: float32 [192], replicated, may hold values from -3 to 3
- gain_lift: float32 [192], replicated, may hold values from 0.1 to 1.9
- w_final: bfloat16 [3, 3, 192, 96], replicated, may hold values from -0.15625 to 0.15625
- b_final: float32 [96], replicated, may hold values from -3 to 3
Outputs:
- decoded: bfloat16 [64, 128, 49152], P('frames', 'rows')
The draws below stay inside these ranges and needn't reach their ends.
Inputs may be any that keep to these rules, and one draw needn't show every extreme that they name: tile_slot is a permutation of the 16384 canvas slots. Of the 128 tiles that one device holds, at most 2 have slots in the block of one owner (slot // 128), and in every draw each device has exactly 2 for some owner.
All inputs are finite; a program needn't handle non-finite values.
Results may differ from the reference program's by a relative error of at most 0.0055.
Values may be sent and summed in bfloat16 or wider, within the bound.
A program may use at most 128 MiB of HBM per device.

```python
import jax
import jax.numpy as jnp
from jax import lax

C_LAT = 16
C1 = 384
C2 = 192
C3 = 96
TILE_PX = 8
FR_DEV = 2
ROWS_DEV = 4
WIDTH = 128
FRAMES = 32
HEIGHT = 32
SLOTS = 128
TILES = 16384
CAP = 2
N_ROWS = 8
N_FRAMES = 16
DEVICES = 128


def draw_tile_slot(key, part):
    key = jax.random.fold_in(key, 11)
    key_shift, key_source, key_owner, key_pack, key_place = jax.random.split(key, 5)
    others = 1 + jnp.arange((DEVICES - 1) * CAP, dtype=jnp.int32) // CAP
    picked = jax.random.permutation(key_shift, others)[:SLOTS - CAP]
    shifts = jnp.concatenate([jnp.zeros((CAP,), jnp.int32), picked])
    source_perm = jax.random.permutation(key_source, DEVICES).astype(jnp.int32)
    owner_perm = jax.random.permutation(key_owner, DEVICES).astype(jnp.int32)
    base = jnp.arange(DEVICES, dtype=jnp.int32)
    owner_pos = (base[:, None] + shifts[None, :]) % DEVICES
    owner_dev = owner_perm[owner_pos]
    place_keys = jax.random.split(key_place, DEVICES)
    placing = jax.vmap(lambda single_key: jax.random.permutation(single_key, SLOTS))(place_keys).astype(jnp.int32)
    inside = placing[owner_pos, jnp.arange(SLOTS, dtype=jnp.int32)[None, :]]
    target = owner_dev * SLOTS + inside
    pack_keys = jax.random.split(key_pack, DEVICES)
    arranged = jax.vmap(lambda single_key: jax.random.permutation(single_key, SLOTS))(pack_keys).astype(jnp.int32)
    position = source_perm[:, None] * SLOTS + arranged
    return jnp.zeros((TILES,), jnp.int32).at[position.reshape(-1)].set(target.reshape(-1))


def block_scale(own_key, shape, cuts, smallest, high):
    def one(dim, shards_of):
        steps = jax.random.uniform(jax.random.fold_in(jax.random.fold_in(own_key, 6), dim), (shards_of,), jnp.float32, smallest / len(cuts), high / len(cuts))
        return jnp.repeat(jnp.exp(steps), shape[dim] // shards_of).reshape((-1,) + (1,) * (len(shape) - dim - 1))

    level = one(*cuts[0])
    for cut in cuts[1:]:
        level = level * one(*cut)
    return level


def normal_values(own_key, extent, deviation, reach, cuts=(), kind=jnp.bfloat16):
    values = deviation * jax.random.normal(own_key, extent, jnp.float32)
    if cuts:
        values = values * block_scale(own_key, extent, cuts, -0.22, 0.18)
    return jnp.clip(values, -reach, reach).astype(kind)


def setup_inputs(seed: int = 0) -> dict:
    arg_keys = jax.random.split(jax.random.key(seed), 13)
    return {
        "latents": normal_values(arg_keys[0], (TILES, TILE_PX * C_LAT), 1.0, 6.0, ((0, 128),)),
        "tile_slot": draw_tile_slot(jax.random.fold_in(arg_keys[12], 71), 0),
        "w_in": normal_values(arg_keys[2], (3, 3, 3, C_LAT, C1), (27 * C_LAT) ** -0.5, 0.3125),
        "b_in": normal_values(arg_keys[3], (C1,), 0.5, 3.0, (), jnp.float32),
        "gain_in": jnp.clip(1.0 + 0.18 * jax.random.normal(arg_keys[4], (C1,), jnp.float32), 0.1, 1.9),
        "w_time": normal_values(arg_keys[5], (3, C1, 2 * C1), (3 * C1) ** -0.5, 0.1875),
        "b_time": normal_values(arg_keys[6], (2 * C1,), 0.5, 3.0, (), jnp.float32),
        "w_lift": normal_values(arg_keys[7], (3, 3, C1, C2), (9 * C1) ** -0.5, 0.109375),
        "b_lift": normal_values(arg_keys[8], (C2,), 0.5, 3.0, (), jnp.float32),
        "gain_lift": jnp.clip(1.0 + 0.18 * jax.random.normal(arg_keys[9], (C2,), jnp.float32), 0.1, 1.9),
        "w_final": normal_values(arg_keys[10], (3, 3, C2, C3), (9 * C2) ** -0.5, 0.15625),
        "b_final": normal_values(arg_keys[11], (C3,), 0.5, 3.0, (), jnp.float32),
    }


def norm_silu(values, gain):
    factor = lax.rsqrt(lax.optimization_barrier(jnp.mean(values * values, axis=-1, keepdims=True)) + 1e-06)
    normed = values * factor * gain
    return normed * jax.nn.sigmoid(normed)

def conv_plane(values, weight):
    return lax.conv_general_dilated(values, weight, (1, 1), 'VALID', dimension_numbers=('NHWC', 'HWIO', 'NHWC'), preferred_element_type=jnp.float32)

def conv_volume(values, weight):
    return lax.conv_general_dilated(values, weight, (1, 1, 1), 'VALID', dimension_numbers=('NDHWC', 'DHWIO', 'NDHWC'), preferred_element_type=jnp.float32)

def nearest_double(values):
    return jnp.repeat(jnp.repeat(values, 2, axis=0), 2, axis=1)

def reference(latents, tile_slot, w_in, b_in, gain_in, w_time, b_time, w_lift, b_lift, gain_lift, w_final, b_final):
    canvas = jnp.zeros((TILES, TILE_PX * C_LAT), latents.dtype).at[tile_slot].set(latents)
    latent_grid = canvas.reshape(N_ROWS, N_FRAMES, FR_DEV, ROWS_DEV, WIDTH * C_LAT)
    latent_grid = latent_grid.transpose(1, 2, 0, 3, 4).reshape(FRAMES, HEIGHT, WIDTH, C_LAT)
    padded = jnp.pad(latent_grid, ((2, 0), (1, 1), (1, 1), (0, 0)))
    hidden = conv_volume(padded[None], w_in)[0] + b_in
    features = norm_silu(hidden, gain_in).astype(jnp.bfloat16)
    history = jnp.pad(features, ((2, 0), (0, 0), (0, 0), (0, 0)))
    temporal = b_time + jnp.zeros((FRAMES * HEIGHT * WIDTH, 2 * C1), jnp.float32)
    for offset in range(3):
        temporal = temporal + jnp.dot(history[offset:offset + FRAMES].reshape(-1, C1), w_time[offset], preferred_element_type=jnp.float32)
    doubled = temporal.reshape(FRAMES, HEIGHT, WIDTH, 2, C1).transpose(0, 3, 1, 2, 4)
    doubled = doubled.reshape(2 * FRAMES, HEIGHT, WIDTH, C1).astype(jnp.bfloat16)

    def decode_frame(single_frame):
        raised = jnp.pad(nearest_double(single_frame), ((1, 1), (1, 1), (0, 0)))
        middle = conv_plane(raised[None], w_lift)[0] + b_lift
        second = norm_silu(middle, gain_lift).astype(jnp.bfloat16)
        lifted = jnp.pad(nearest_double(second), ((1, 1), (1, 1), (0, 0)))
        result = conv_plane(lifted[None], w_final)[0] + b_final
        return result.astype(jnp.bfloat16).reshape(4 * HEIGHT, 4 * WIDTH * C3)
    return lax.map(decode_frame, doubled)
```

```python
import functools

import jax
import jax.numpy as jnp
from jax import lax
from jax.experimental import pallas as pl
from jax.experimental.pallas import tpu as pltpu
from jax.sharding import PartitionSpec as P

BF16, F32 = jnp.bfloat16, jnp.float32
XB = 16
SC = 4


def silu(n):
    half = 0.5 * n
    return half + half * jnp.tanh(half)


def pick(parts, tap, phase):
    if phase == 0:
        return parts[0] + parts[1] if tap == 0 else parts[2]
    return parts[0] if tap == 0 else parts[1] + parts[2]


def summed_taps(load, ty, tx, py, px):
    rows = [pick([load(dy, dx) for dy in range(3)], ty, py) for dx in range(3)]
    return pick(rows, tx, px)


def weights_kernel(win_ref, wlift_ref, wfinal_ref, band_ref, lift_ref, final_ref):
    channels = win_ref.shape[-1]
    band_ref[...] = jnp.zeros_like(band_ref)
    for k in range(3):
        for dy in range(3):
            for dx in range(3):
                taps = win_ref[k, dy, dx]
                for pp in range(2):
                    row = 256 * k + 64 * dy + 16 * (dx + pp)
                    band_ref[row : row + 16, channels * pp : channels * (pp + 1)] = taps
    depth = wlift_ref.shape[2]

    def lift_rows(step, carry):
        row = pl.multiple_of(step * 64, 64)

        def wide(dy, dx):
            return wlift_ref[dy, dx, pl.ds(row, 64), 0:128].astype(F32)

        def narrow(dy, dx):
            return wlift_ref[dy, dx, pl.ds(row, 64), 128:192].astype(F32)

        for ty in range(2):
            for tx in range(2):
                for px in range(2):
                    tiles = [
                        summed_taps(wide, ty, tx, 0, px),
                        jnp.concatenate([summed_taps(narrow, ty, tx, py, px) for py in range(2)], axis=-1),
                        summed_taps(wide, ty, tx, 1, px),
                    ]
                    for n, tile in enumerate(tiles):
                        lane = 384 * px + 128 * n
                        lift_ref[pl.ds(depth * (2 * ty + tx) + row, 64), lane : lane + 128] = tile.astype(BF16)
        return carry

    lax.fori_loop(0, depth // 64, lift_rows, 0)

    def final_rows(part):
        rows = slice(64 * part, 64 * (part + 1))
        low = lax.broadcasted_iota(jnp.int32, (64, 128), 1) < 64
        pad = jnp.zeros((64, 32), F32)

        def load(dy, dx):
            return wfinal_ref[dy, dx, rows, :].astype(F32)

        for ty in range(2):
            for tx in range(2):
                for qy in range(2):
                    q0, q1 = (
                        jnp.concatenate([summed_taps(load, ty, tx, qy, qx), pad], axis=-1) for qx in range(2)
                    )
                    r0, r1 = pltpu.roll(q0, 96, 1), pltpu.roll(q1, 64, 1)
                    pairs = (
                        (jnp.where(low, r1, r0), jnp.where(low, r0, r1)),
                        (pltpu.roll(q0, 32, 1), q1),
                    )
                    for xpar, tiles in enumerate(pairs):
                        px = tx if xpar else 1 - tx
                        for jpar in range(2):
                            py = ty if jpar else 1 - ty
                            slot = 384 * px
                            if part < 2:
                                slot += 256 * py + 64 * part
                            else:
                                slot += 128 + 64 * py
                            for n, tile in enumerate(tiles):
                                lane = 256 * qy + 128 * n
                                final_ref[2 * jpar + xpar, slot : slot + 64, lane : lane + 128] = tile.astype(BF16)

    for part in range(3):
        final_rows(part)


def make_weights(w_in, w_lift, w_final):
    whole = pl.BlockSpec(memory_space=pltpu.VMEM)
    return pl.pallas_call(
        weights_kernel,
        in_specs=[whole] * 3,
        out_specs=[whole] * 3,
        out_shape=[
            jax.ShapeDtypeStruct((768, 768), BF16),
            jax.ShapeDtypeStruct((1536, 768), BF16),
            jax.ShapeDtypeStruct((4, 768, 512), BF16),
        ],
        compiler_params=pltpu.CompilerParams(vmem_limit_bytes=48 * 1024 * 1024),
        name="weights",
    )(w_in, w_lift, w_final)


def front(place_ref, blocks_ref, band_ref, bin_ref, gin_ref, wtime_ref, btime_ref, grid_ref, dbl_ref):
    row, frame = place_ref[0], place_ref[1]
    top, bottom = row == 0, row == place_ref[2] - 1
    out_row = lax.broadcasted_iota(jnp.int32, (256, 384), 0)
    in_row = lax.broadcasted_iota(jnp.int32, (256, 384), 1)
    y_in = out_row % 8 + 2
    wanted = (y_in // 4) * 128 + (out_row // 128) * 64 + (y_in % 4) * 16 + (out_row // 8) % 16
    inside = jnp.logical_and(
        jnp.logical_or(jnp.logical_not(top), y_in >= 4), jnp.logical_or(jnp.logical_not(bottom), y_in < 8)
    )
    chosen = jnp.logical_and(in_row == wanted, inside)
    zero_col = jnp.zeros((6, 1, 8, 128), F32)
    grid_ref[:, 0:1] = zero_col
    grid_ref[:, 17:18] = zero_col
    for part in range(3):
        select = jnp.where(jnp.logical_and(chosen, frame + part >= 2), 1.0, 0.0).astype(BF16)
        cells = blocks_ref[part].reshape(384, 128)
        picked = jnp.dot(select, cells, preferred_element_type=F32)
        grid_ref[2 * part : 2 * part + 2, 1:17] = picked.reshape(2, 16, 8, 128)

    lane = lax.broadcasted_iota(jnp.int32, (1, 1, 1, 128), 3)
    sub = lax.broadcasted_iota(jnp.int32, (1, 1, 8, 1), 2)
    edge_col = jnp.zeros((1, 16, 384), BF16)
    for v in range(3):
        dbl_ref[v, 0:1] = edge_col
        dbl_ref[v, dbl_ref.shape[1] - 1 :] = edge_col

    def chunk(step, carry):
        s0 = step * SC
        cells = grid_ref[:, pl.ds(s0, SC + 2)]
        flat = cells.reshape(6 * (SC + 2), 8, 128)
        turned = [pltpu.roll(flat, 1, 1), flat, pltpu.roll(flat, 7, 1)]
        pieces = []
        for q in range(4):
            shift = (16 - 32 * q) % 128
            parts = []
            for d, lanes in enumerate((shift, shift + 64, shift)):
                moved = pltpu.roll(turned[d], lanes % 128, 2).reshape(6, SC + 2, 8, 128)
                own = moved[:, 1:-1]
                at = 64 * (d % 2)
                if q == 0:
                    own = jnp.where((lane >= at) & (lane < at + 16), moved[:, :-2], own)
                if q == 3:
                    own = jnp.where((lane >= at + 48) & (lane < at + 64), moved[:, 2:], own)
                parts.append(own)
            first = jnp.where(lane < 64, parts[0], parts[1])
            pieces.append(jnp.concatenate([first, parts[2]], axis=-1))
        patch = jnp.stack(pieces, axis=2).reshape(6, SC * 4 * 8, 256).astype(BF16)
        patch = jnp.concatenate([patch[k : k + 4] for k in range(3)], axis=-1)
        hidden = jnp.dot(patch.reshape(4 * SC * 32, 768), band_ref[...], preferred_element_type=F32)
        halves = []
        for pp in range(2):
            h = hidden[:, 384 * pp : 384 * (pp + 1)] + bin_ref[...]
            mean = jnp.sum(h * h, axis=-1, keepdims=True) * (1.0 / 384)
            v = silu(h * lax.rsqrt(mean + 1e-6) * gin_ref[...])
            halves.append(v.reshape(4, SC * 4, 8, 384))
        feats = jnp.stack(halves, axis=2)
        t_in = lax.broadcasted_iota(jnp.int32, (4, 1, 1, 1, 1), 0)
        feats = jnp.where(t_in + 2 * frame >= 2, feats, 0.0)
        feats = feats.reshape(4, SC * 64, 384).astype(BF16)
        hist = jnp.concatenate([feats[k : k + 2] for k in range(3)], axis=-1)
        acc = jnp.dot(hist.reshape(2 * SC * 64, 1152), wtime_ref[...], preferred_element_type=F32)
        acc = acc + btime_ref[...]
        acc = acc.reshape(2, SC * 8, 8, 768)
        for v in range(3):
            both = []
            for j in range(2):
                a0 = pltpu.roll(acc[0, :, :, 384 * j : 384 * (j + 1)], 7 - v, 1)
                a1 = pltpu.roll(acc[1, :, :, 384 * j : 384 * (j + 1)], 3 - v, 1)
                both.append(jnp.where(sub[0] < 4, a0, a1))
            full = jnp.concatenate(both, axis=1)
            group = lax.broadcasted_iota(jnp.int32, (1, 16, 1), 1) % 4
            if v == 0:
                full = jnp.where(jnp.logical_and(top, group == 0), 0.0, full)
            if v == 2:
                full = jnp.where(jnp.logical_and(bottom, group == 3), 0.0, full)
            dbl_ref[v, pl.ds(8 * s0 + 1, SC * 8)] = full.astype(BF16)
        return carry

    lax.fori_loop(0, 16 // SC, chunk, 0)


def back(step, place_ref, dbl_ref, wl_ref, bl_ref, gl_ref, wf_ref, bf_ref, out_ref, rows_ref):
    top, bottom = place_ref[0] == 0, place_ref[0] == place_ref[2] - 1
    width = dbl_ref.shape[1] - 2
    x0 = step * XB
    count = XB + 1
    lane = lax.broadcasted_iota(jnp.int32, (1, 1, 128), 2)
    low = lane < 64
    d_m, d_0, d_p = (dbl_ref[v, pl.ds(x0, XB + 2)] for v in range(3))
    group = lax.broadcasted_iota(jnp.int32, (1, 16, 1), 1) % 4
    col = lax.broadcasted_iota(jnp.int32, (count, 1, 1), 0) + (x0 - 1)

    def lift(upper, lower, drop):
        patch = jnp.concatenate([upper[:-1], upper[1:], lower[:-1], lower[1:]], axis=-1)
        acc = jnp.dot(patch.reshape(count * 16, -1), wl_ref[...], preferred_element_type=F32)
        acc = acc.reshape(count, 16, 768) + bl_ref[...]
        out = []
        for px in range(2):
            tiles = [acc[..., 384 * px + 128 * k : 384 * px + 128 * (k + 1)] for k in range(3)]
            sq = [v * v for v in tiles]
            s0 = jnp.sum(sq[0] + jnp.where(low, sq[1], 0.0), axis=-1, keepdims=True)
            s1 = jnp.sum(sq[2] + jnp.where(low, 0.0, sq[1]), axis=-1, keepdims=True)
            f0 = lax.rsqrt(s0 * (1.0 / 192) + 1e-6)
            f1 = lax.rsqrt(s1 * (1.0 / 192) + 1e-6)
            inside = (col >= 0) if px == 0 else (col < width - 1)
            for k, f in enumerate((f0, jnp.where(low, f0, f1), f1)):
                v = silu(tiles[k] * f * gl_ref[:, 384 * px + 128 * k : 384 * px + 128 * (k + 1)])
                keep = inside if drop[k] is None else jnp.logical_and(inside, jnp.logical_not(drop[k]))
                out.append(jnp.where(keep, v, 0.0).astype(BF16))
        return out

    above = jnp.logical_and(group == 0, top)
    below = jnp.logical_and(group == 3, bottom)
    s_m = lift(d_m, d_0, (above, jnp.logical_and(above, low), None))
    s_p = lift(d_0, d_p, (None, jnp.logical_and(below, jnp.logical_not(low)), below))
    s_e = []
    for px in range(2):
        s_e += [s_p[3 * px], jnp.where(low, s_p[3 * px + 1], s_m[3 * px + 1]), s_m[3 * px + 2]]

    def odd(tiles):
        return jnp.concatenate(tiles, axis=-1).reshape(count * 16, 768)

    def even(tiles):
        return jnp.concatenate([v[1:] for v in tiles[:3]] + [v[:-1] for v in tiles[3:]], axis=-1).reshape(XB * 16, 768)

    def mul(lhs, kind, lo, hi):
        return jnp.dot(lhs, wf_ref[kind, :, lo:hi], preferred_element_type=F32).reshape(-1, 16, hi - lo)

    e_o, e_e = mul(odd(s_e), 1, 0, 512), mul(even(s_e), 0, 0, 512)
    results = (
        (mul(odd(s_m), 3, 256, 512), mul(even(s_m), 2, 256, 512)),
        (e_o[..., :256], e_e[..., :256]),
        (e_o[..., 256:], e_e[..., 256:]),
        (mul(odd(s_p), 3, 0, 256), mul(even(s_p), 2, 0, 256)),
    )
    for a, (o, e) in enumerate(results):
        t0 = jnp.where(lane < 96, o[:-1, :, 128:], e[..., :128])
        t1 = e[..., 128:]
        t2 = jnp.where(lane < 32, e[..., :128], o[1:, :, :128])
        for k, t in enumerate((t0, t1, t2)):
            t = t + bf_ref[:, 128 * k : 128 * (k + 1)]
            for u in range(XB):
                rows_ref[3 * u + k, pl.ds(a, 16, stride=4), :] = t[u]
    for j in range(2):
        for t in range(2):
            base = 16 * (2 * j + t)
            for n in range(3 * XB):
                out_ref[2 * t + j, :, 128 * n : 128 * (n + 1)] = rows_ref[n, base : base + 16, :].astype(BF16)


def decode_kernel(
    place_ref, blocks_ref, band_ref, bin_ref, gin_ref, wtime_ref, btime_ref, wl_ref, bl_ref, gl_ref, wf_ref, bf_ref,
    out_ref, grid_ref, dbl_ref, rows_ref,
):
    step = pl.program_id(0)

    @pl.when(step == 0)
    def _():
        front(place_ref, blocks_ref, band_ref, bin_ref, gin_ref, wtime_ref, btime_ref, grid_ref, dbl_ref)

    back(step, place_ref, dbl_ref, wl_ref, bl_ref, gl_ref, wf_ref, bf_ref, out_ref, rows_ref)


def lanes_of_phases(v):
    half = jnp.concatenate([v[:128], v[128:], v[128:], v[:128]])
    return jnp.concatenate([half, half])[None]


def decode(place, blocks, band, wl, wf, b_in, gain_in, w_time, b_time, b_lift, gain_lift, b_final):
    width = 128
    args = (
        blocks, band, b_in[None], gain_in[None], w_time.reshape(1152, 768), b_time[None],
        wl, lanes_of_phases(b_lift), lanes_of_phases(gain_lift), wf, jnp.tile(b_final, 4)[None],
    )

    def whole(a):
        return pl.BlockSpec(a.shape, lambda i: (0,) * a.ndim, pipeline_mode=pl.Buffered(1))

    return pl.pallas_call(
        decode_kernel,
        grid=(width // XB,),
        in_specs=[pl.BlockSpec(memory_space=pltpu.SMEM)] + [whole(a) for a in args],
        out_specs=pl.BlockSpec((4, 16, XB * 384), lambda i: (0, 0, i)),
        out_shape=jax.ShapeDtypeStruct((4, 16, width * 384), BF16),
        scratch_shapes=[
            pltpu.VMEM((6, 18, 8, 128), F32),
            pltpu.VMEM((3, width + 2, 16, 384), BF16),
            pltpu.VMEM((XB * 3, 64, 128), F32),
        ],
        compiler_params=pltpu.CompilerParams(vmem_limit_bytes=56 * 1024 * 1024),
        name="decode",
    )(place, *args)


def turned(block, axis, distance):
    count = lax.axis_size(axis)
    return lax.ppermute(block, axis, [(i, (i + distance) % count) for i in range(count)])


def exchange(latents, tile_slot):
    devices = lax.axis_size("rows") * lax.axis_size("frames")
    slots, width = latents.shape
    owner, inside = tile_slot // slots, tile_slot % slots
    same = owner[:, None] == owner[None, :]
    earlier = jnp.arange(slots)[None, :] < jnp.arange(slots)[:, None]
    rank = jnp.sum(jnp.where(same & earlier, 1, 0), axis=1)
    target = 2 * owner + rank
    pack = (jnp.arange(2 * devices)[:, None] == target[None, :]).astype(BF16)
    tagged = jnp.concatenate([latents, jnp.broadcast_to((inside + 1).astype(BF16)[:, None], (slots, width))], axis=1)
    outgoing = jnp.dot(pack, tagged).reshape(devices, 4 * width)
    arrived = lax.all_to_all(outgoing, ("rows", "frames"), split_axis=0, concat_axis=0, tiled=True)
    arrived = arrived.reshape(2 * devices, 2 * width)
    place = (jnp.arange(1, slots + 1, dtype=jnp.int32)[:, None] == arrived[:, width].astype(jnp.int32)[None, :]).astype(BF16)
    own = jnp.dot(place, arrived[:, :width])
    frames = jnp.stack([turned(own, "frames", 2), turned(own, "frames", 1), own])
    return jnp.stack([turned(frames, "rows", 1), frames, turned(frames, "rows", -1)], axis=1)


def shards(
    latents, tile_slot, w_in, b_in, gain_in, w_time, b_time, w_lift, b_lift, gain_lift, w_final, b_final
):
    place = jnp.stack([lax.axis_index("rows"), lax.axis_index("frames"), lax.axis_size("rows")]).astype(jnp.int32)
    band, wl, wf = make_weights(w_in, w_lift, w_final)
    blocks = exchange(latents, tile_slot)
    return decode(place, blocks, band, wl, wf, b_in, gain_in, w_time, b_time, b_lift, gain_lift, b_final)


def solution(mesh):
    in_specs = (P(("rows", "frames"), None), P(("rows", "frames"))) + (P(),) * 10
    out_specs = P("frames", "rows", None)
    return jax.shard_map(shards, mesh=mesh, in_specs=in_specs, out_specs=out_specs, check_vma=False)
```

```python
import functools

import jax
import jax.numpy as jnp
from jax import lax
from jax.experimental import pallas as pl
from jax.experimental.pallas import tpu as pltpu
from jax.sharding import PartitionSpec as P

BF16, F32 = jnp.bfloat16, jnp.float32
XB = 16
SC = 4


def silu(n):
    half = 0.5 * n
    return half + half * jnp.tanh(half)


def pick(parts, tap, phase):
    if phase == 0:
        return parts[0] + parts[1] if tap == 0 else parts[2]
    return parts[0] if tap == 0 else parts[1] + parts[2]


def summed_taps(load, ty, tx, py, px):
    rows = [pick([load(dy, dx) for dy in range(3)], ty, py) for dx in range(3)]
    return pick(rows, tx, px)


def make_band(win_ref, band_ref):
    channels = win_ref.shape[-1]
    band_ref[...] = jnp.zeros_like(band_ref)
    for k in range(3):
        for dy in range(3):
            for dx in range(3):
                taps = win_ref[k, dy, dx]
                for pp in range(2):
                    row = 256 * k + 64 * dy + 16 * (dx + pp)
                    band_ref[row : row + 16, channels * pp : channels * (pp + 1)] = taps


def make_lift(wlift_ref, lift_ref, ty, tx):
    depth = wlift_ref.shape[-1]

    def part(lo, hi, py, px):
        return summed_taps(lambda dy, dx: wlift_ref[dy, dx, lo:hi, :].astype(F32), ty, tx, py, px)

    for px in range(2):
        tiles = [
            part(0, 128, 0, px),
            jnp.concatenate([part(128, 192, 0, px), part(128, 192, 1, px)], axis=0),
            part(0, 128, 1, px),
        ]
        for n, tile in enumerate(tiles):
            lane = 384 * px + 128 * n
            row = depth * (2 * ty + tx)
            lift_ref[row : row + depth, lane : lane + 128] = tile.T.astype(BF16)


def make_final(wfinal_ref, final_ref, part):
    rows = slice(64 * part, 64 * (part + 1))
    low = lax.broadcasted_iota(jnp.int32, (64, 128), 1) < 64
    pad = jnp.zeros((64, 32), F32)

    def load(dy, dx):
        return wfinal_ref[dy, dx, rows, :].astype(F32)

    for ty in range(2):
        for tx in range(2):
            for qy in range(2):
                q0, q1 = (jnp.concatenate([summed_taps(load, ty, tx, qy, qx), pad], axis=-1) for qx in range(2))
                r0, r1 = pltpu.roll(q0, 96, 1), pltpu.roll(q1, 64, 1)
                pairs = ((jnp.where(low, r1, r0), jnp.where(low, r0, r1)), (pltpu.roll(q0, 32, 1), q1))
                for xpar, tiles in enumerate(pairs):
                    px = tx if xpar else 1 - tx
                    for jpar in range(2):
                        py = ty if jpar else 1 - ty
                        slot = 384 * px + (256 * py + 64 * part if part < 2 else 128 + 64 * py)
                        for n, tile in enumerate(tiles):
                            lane = 256 * qy + 128 * n
                            final_ref[2 * jpar + xpar, slot : slot + 64, lane : lane + 128] = tile.astype(BF16)


def front(blocks_ref, band_ref, bin_ref, gin_ref, wtime_ref, btime_ref, grid_ref, dbl_ref):
    row, frame = lax.axis_index("rows"), lax.axis_index("frames")
    top, bottom = row == 0, row == lax.axis_size("rows") - 1
    out_row = lax.broadcasted_iota(jnp.int32, (256, 256), 0)
    in_row = lax.broadcasted_iota(jnp.int32, (256, 256), 1)
    t, s, y = out_row // 128, (out_row // 8) % 16, out_row % 8
    wanted = jnp.where(
        y < 2,
        32 * t + 16 * y + s,
        jnp.where(y < 6, 64 + 64 * t + 16 * (y - 2) + s, 192 + 32 * t + 16 * (y - 6) + s),
    )
    inside = jnp.logical_and(
        jnp.logical_or(jnp.logical_not(top), y >= 2), jnp.logical_or(jnp.logical_not(bottom), y < 6)
    )
    chosen = jnp.logical_and(in_row == wanted, inside)
    zero_col = jnp.zeros((6, 1, 8, 128), F32)
    grid_ref[:, 0:1] = zero_col
    grid_ref[:, 17:18] = zero_col
    for part in range(3):
        select = jnp.where(jnp.logical_and(chosen, frame + part >= 2), 1.0, 0.0).astype(BF16)
        picked = jnp.dot(select, blocks_ref[part], preferred_element_type=F32)
        grid_ref[2 * part : 2 * part + 2, 1:17] = picked.reshape(2, 16, 8, 128)

    lane = lax.broadcasted_iota(jnp.int32, (1, 1, 1, 128), 3)
    sub = lax.broadcasted_iota(jnp.int32, (1, 1, 8, 1), 2)
    edge_col = jnp.zeros((1, 16, 384), BF16)
    for v in range(3):
        dbl_ref[v, 0:1] = edge_col
        dbl_ref[v, dbl_ref.shape[1] - 1 :] = edge_col

    def chunk(step, carry):
        s0 = step * SC
        cells = grid_ref[:, pl.ds(s0, SC + 2)]
        flat = cells.reshape(6 * (SC + 2), 8, 128)
        turned = [pltpu.roll(flat, 1, 1), flat, pltpu.roll(flat, 7, 1)]
        pieces = []
        for q in range(4):
            shift = (16 - 32 * q) % 128
            parts = []
            for d, lanes in enumerate((shift, shift + 64, shift)):
                moved = pltpu.roll(turned[d], lanes % 128, 2).reshape(6, SC + 2, 8, 128)
                own = moved[:, 1:-1]
                at = 64 * (d % 2)
                if q == 0:
                    own = jnp.where((lane >= at) & (lane < at + 16), moved[:, :-2], own)
                if q == 3:
                    own = jnp.where((lane >= at + 48) & (lane < at + 64), moved[:, 2:], own)
                parts.append(own)
            first = jnp.where(lane < 64, parts[0], parts[1])
            pieces.append(jnp.concatenate([first, parts[2]], axis=-1))
        patch = jnp.stack(pieces, axis=2).reshape(6, SC * 4 * 8, 256).astype(BF16)
        patch = jnp.concatenate([patch[k : k + 4] for k in range(3)], axis=-1)
        hidden = jnp.dot(patch.reshape(4 * SC * 32, 768), band_ref[...], preferred_element_type=F32)
        halves = []
        for pp in range(2):
            h = hidden[:, 384 * pp : 384 * (pp + 1)] + bin_ref[...]
            mean = jnp.sum(h * h, axis=-1, keepdims=True) * (1.0 / 384)
            v = silu(h * lax.rsqrt(mean + 1e-6) * gin_ref[...])
            halves.append(v.reshape(4, SC * 4, 8, 384))
        feats = jnp.stack(halves, axis=2)
        t_in = lax.broadcasted_iota(jnp.int32, (4, 1, 1, 1, 1), 0)
        feats = jnp.where(t_in + 2 * frame >= 2, feats, 0.0)
        feats = feats.reshape(4, SC * 64, 384).astype(BF16)
        hist = jnp.concatenate([feats[k : k + 2] for k in range(3)], axis=-1)
        acc = jnp.dot(hist.reshape(2 * SC * 64, 1152), wtime_ref[...], preferred_element_type=F32)
        acc = acc + btime_ref[...]
        acc = acc.reshape(2, SC * 8, 8, 768)
        for v in range(3):
            both = []
            for j in range(2):
                a0 = pltpu.roll(acc[0, :, :, 384 * j : 384 * (j + 1)], 7 - v, 1)
                a1 = pltpu.roll(acc[1, :, :, 384 * j : 384 * (j + 1)], 3 - v, 1)
                both.append(jnp.where(sub[0] < 4, a0, a1))
            full = jnp.concatenate(both, axis=1)
            group = lax.broadcasted_iota(jnp.int32, (1, 16, 1), 1) % 4
            if v == 0:
                full = jnp.where(jnp.logical_and(top, group == 0), 0.0, full)
            if v == 2:
                full = jnp.where(jnp.logical_and(bottom, group == 3), 0.0, full)
            dbl_ref[v, pl.ds(8 * s0 + 1, SC * 8)] = full.astype(BF16)
        return carry

    lax.fori_loop(0, 16 // SC, chunk, 0)


def back(step, dbl_ref, wl_ref, bl_ref, gl_ref, wf_ref, bf_ref, out_ref, rows_ref):
    row = lax.axis_index("rows")
    top, bottom = row == 0, row == lax.axis_size("rows") - 1
    width = dbl_ref.shape[1] - 2
    x0 = step * XB
    count = XB + 1
    lane = lax.broadcasted_iota(jnp.int32, (1, 1, 128), 2)
    low = lane < 64
    d_m, d_0, d_p = (dbl_ref[v, pl.ds(x0, XB + 2)] for v in range(3))
    group = lax.broadcasted_iota(jnp.int32, (1, 16, 1), 1) % 4
    col = lax.broadcasted_iota(jnp.int32, (count, 1, 1), 0) + (x0 - 1)

    def lift(upper, lower, drop):
        patch = jnp.concatenate([upper[:-1], upper[1:], lower[:-1], lower[1:]], axis=-1)
        acc = jnp.dot(patch.reshape(count * 16, -1), wl_ref[...], preferred_element_type=F32)
        acc = acc.reshape(count, 16, 768) + bl_ref[...]
        out = []
        for px in range(2):
            tiles = [acc[..., 384 * px + 128 * k : 384 * px + 128 * (k + 1)] for k in range(3)]
            sq = [v * v for v in tiles]
            s0 = jnp.sum(sq[0] + jnp.where(low, sq[1], 0.0), axis=-1, keepdims=True)
            s1 = jnp.sum(sq[2] + jnp.where(low, 0.0, sq[1]), axis=-1, keepdims=True)
            f0 = lax.rsqrt(s0 * (1.0 / 192) + 1e-6)
            f1 = lax.rsqrt(s1 * (1.0 / 192) + 1e-6)
            inside = (col >= 0) if px == 0 else (col < width - 1)
            for k, f in enumerate((f0, jnp.where(low, f0, f1), f1)):
                v = silu(tiles[k] * f * gl_ref[:, 384 * px + 128 * k : 384 * px + 128 * (k + 1)])
                keep = inside if drop[k] is None else jnp.logical_and(inside, jnp.logical_not(drop[k]))
                out.append(jnp.where(keep, v, 0.0).astype(BF16))
        return out

    above = jnp.logical_and(group == 0, top)
    below = jnp.logical_and(group == 3, bottom)
    s_m = lift(d_m, d_0, (above, jnp.logical_and(above, low), None))
    s_p = lift(d_0, d_p, (None, jnp.logical_and(below, jnp.logical_not(low)), below))
    s_e = []
    for px in range(2):
        s_e += [s_p[3 * px], jnp.where(low, s_p[3 * px + 1], s_m[3 * px + 1]), s_m[3 * px + 2]]

    def odd(tiles):
        return jnp.concatenate(tiles, axis=-1).reshape(count * 16, 768)

    def even(tiles):
        return jnp.concatenate([v[1:] for v in tiles[:3]] + [v[:-1] for v in tiles[3:]], axis=-1).reshape(XB * 16, 768)

    def mul(lhs, kind, lo, hi):
        return jnp.dot(lhs, wf_ref[kind, :, lo:hi], preferred_element_type=F32).reshape(-1, 16, hi - lo)

    e_o, e_e = mul(odd(s_e), 1, 0, 512), mul(even(s_e), 0, 0, 512)
    results = (
        (mul(odd(s_m), 3, 256, 512), mul(even(s_m), 2, 256, 512)),
        (e_o[..., :256], e_e[..., :256]),
        (e_o[..., 256:], e_e[..., 256:]),
        (mul(odd(s_p), 3, 0, 256), mul(even(s_p), 2, 0, 256)),
    )
    for a, (o, e) in enumerate(results):
        t0 = jnp.where(lane < 96, o[:-1, :, 128:], e[..., :128])
        t1 = e[..., 128:]
        t2 = jnp.where(lane < 32, e[..., :128], o[1:, :, :128])
        for k, t in enumerate((t0, t1, t2)):
            t = t + bf_ref[:, 128 * k : 128 * (k + 1)]
            for u in range(XB):
                rows_ref[3 * u + k, pl.ds(a, 16, stride=4), :] = t[u]
    for j in range(2):
        for t in range(2):
            base = 16 * (2 * j + t)
            for n in range(3 * XB):
                out_ref[2 * t + j, :, 128 * n : 128 * (n + 1)] = rows_ref[n, base : base + 16, :].astype(BF16)


def decode_kernel(
    blocks_ref, band_ref, bin_ref, gin_ref, wtime_ref, btime_ref, wl_ref, bl_ref, gl_ref, wf_ref, bf_ref,
    out_ref, grid_ref, dbl_ref, rows_ref,
):
    step = pl.program_id(0)

    @pl.when(step == 0)
    def _():
        front(blocks_ref, band_ref, bin_ref, gin_ref, wtime_ref, btime_ref, grid_ref, dbl_ref)

    back(step, dbl_ref, wl_ref, bl_ref, gl_ref, wf_ref, bf_ref, out_ref, rows_ref)


def lanes_of_phases(v):
    half = jnp.concatenate([v[:128], v[128:], v[128:], v[:128]])
    return jnp.concatenate([half, half])[None]


def decode(blocks, band, wl, wf, b_in, gain_in, w_time, b_time, b_lift, gain_lift, b_final):
    width = 128
    args = (
        blocks, band, b_in[None], gain_in[None], w_time.reshape(1152, 768), b_time[None],
        wl, lanes_of_phases(b_lift), lanes_of_phases(gain_lift), wf, jnp.tile(b_final, 4)[None],
    )

    def whole(a):
        return pl.BlockSpec(a.shape, lambda i: (0,) * a.ndim, pipeline_mode=pl.Buffered(1))

    return pl.pallas_call(
        decode_kernel,
        grid=(width // XB,),
        in_specs=[whole(a) for a in args],
        out_specs=pl.BlockSpec((4, 16, XB * 384), lambda i: (0, 0, i)),
        out_shape=jax.ShapeDtypeStruct((4, 16, width * 384), BF16),
        scratch_shapes=[
            pltpu.VMEM((6, 18, 8, 128), F32),
            pltpu.VMEM((3, width + 2, 16, 384), BF16),
            pltpu.VMEM((XB * 3, 64, 128), F32),
        ],
        compiler_params=pltpu.CompilerParams(vmem_limit_bytes=56 * 1024 * 1024),
        name="decode",
    )(*args)


def exchange_kernel(
    rows, frames,
    lat_ref, slot_ref, win_hbm, wlift_hbm, wfinal_hbm,
    blocks_ref, band_hbm, lift_hbm, final_hbm,
    send1, recv1, send2, recv2, above, own, below, win_ref, wlift_ref, wfinal_ref, band_ref, lift_ref, final_ref,
    load_sem, store_sem, send_sem1, recv_sem1, send_sem2, recv_sem2, send_sem3, recv_sem3,
):
    r, f = lax.axis_index("rows"), lax.axis_index("frames")
    loads = [
        pltpu.make_async_copy(src, dst, load_sem.at[n])
        for n, (src, dst) in enumerate(((win_hbm, win_ref), (wlift_hbm, wlift_ref), (wfinal_hbm, wfinal_ref)))
    ]
    for copy in loads:
        copy.start()

    def at(dr, df):
        return {"rows": lax.rem(r + dr + rows, rows), "frames": lax.rem(f + df + frames, frames)}

    near = [(dr, df) for df in range(3) for dr in (0, 1, -1) if (dr, df) != (0, 0)]
    far = [(dr, df) for dr, df in near if dr != 0 and df != 0]
    barrier = pltpu.get_barrier_semaphore()
    sources = [(k, 0) for k in range(1, rows)] + [(0, k) for k in range(1, frames)] + [(-dr, -df) for dr, df in far]
    for dr, df in sources:
        pl.semaphore_signal(barrier, inc=1, device_id=at(dr, df), device_id_type=pl.DeviceIdType.MESH)

    slots, width = lat_ref.shape
    across = jnp.broadcast_to(slot_ref[...].reshape(1, slots), (slots, slots))
    down = across.T
    index = lax.broadcasted_iota(jnp.int32, (slots, slots), 0)
    lane = lax.broadcasted_iota(jnp.int32, (slots, slots), 1)
    twin = jnp.logical_and(across // slots == down // slots, index < lane)
    rank = jnp.sum(jnp.where(twin, 1, 0), axis=0, keepdims=True)
    target = 2 * (across[:1] // slots) + rank
    total = 2 * rows * frames
    place = lax.broadcasted_iota(jnp.int32, (total, slots), 0) == target
    tags = (down % slots + 1).astype(F32).astype(BF16)
    tagged = jnp.concatenate([lat_ref[...], tags], axis=-1)
    packed = jnp.dot(jnp.where(place, 1.0, 0.0).astype(BF16), tagged, preferred_element_type=F32)
    send1[...] = packed.astype(BF16).reshape(send1.shape)
    recv1[r] = send1[r]
    pl.semaphore_wait(barrier, len(sources))

    def remote(src, dst, send, recv, dr, df):
        return pltpu.make_async_remote_copy(
            src_ref=src, dst_ref=dst, send_sem=send, recv_sem=recv,
            device_id=at(dr, df), device_id_type=pl.DeviceIdType.MESH,
        )

    first = []
    for k in range(1, rows):
        peer, source = lax.rem(r + k, rows), lax.rem(r - k + rows, rows)
        out = remote(send1.at[peer], recv1.at[r], send_sem1.at[k], recv_sem1.at[k], k, 0)
        out.start()
        first.append((out, remote(send1.at[peer], recv1.at[source], send_sem1.at[k], recv_sem1.at[k], k, 0)))
    loads[0].wait()
    make_band(win_ref, band_ref)
    loads[1].wait()
    make_lift(wlift_ref, lift_ref, 0, 0)
    for out, arrival in first:
        arrival.wait_recv()

    o = lax.broadcasted_iota(jnp.int32, (total, total), 0)
    i = lax.broadcasted_iota(jnp.int32, (total, total), 1)
    group = 2 * rows
    regroup = i == ((o // 2) % rows) * (2 * frames) + (o // group) * 2 + o % 2
    moved = jnp.dot(
        jnp.where(regroup, 1.0, 0.0).astype(BF16), recv1[...].reshape(total, 2 * width), preferred_element_type=F32
    )
    send2[...] = moved.astype(BF16).reshape(send2.shape)
    recv2[f] = send2[f]
    second = []
    for k in range(1, frames):
        peer, source = lax.rem(f + k, frames), lax.rem(f - k + frames, frames)
        out = remote(send2.at[peer], recv2.at[f], send_sem2.at[k], recv_sem2.at[k], 0, k)
        out.start()
        second.append((out, remote(send2.at[peer], recv2.at[source], send_sem2.at[k], recv_sem2.at[k], 0, k)))
    make_lift(wlift_ref, lift_ref, 0, 1)
    make_lift(wlift_ref, lift_ref, 1, 0)
    for out, arrival in second:
        arrival.wait_recv()

    arrived = recv2[...].reshape(total, 2 * width)
    want = lax.broadcasted_iota(jnp.int32, (total, slots), 1).astype(F32) + 1.0
    land = jnp.where(arrived[:, width:].astype(F32) == want, 1.0, 0.0).astype(BF16)
    canvas = lax.dot_general(land, arrived[:, :width], (((0,), (0,)), ((), ())), preferred_element_type=F32)
    own[2] = canvas.astype(BF16).reshape(2, 64, width)
    third = []
    for n, (dr, df) in enumerate(near):
        src, region = {
            0: (own.at[2], own),
            1: (own.at[2, :, pl.ds(32, 32)], above),
            -1: (own.at[2, :, pl.ds(0, 32)], below),
        }[dr]
        out = remote(src, region.at[2 - df], send_sem3.at[n], recv_sem3.at[n], dr, df)
        out.start()
        third.append(out)
    make_lift(wlift_ref, lift_ref, 1, 1)
    loads[2].wait()
    for part in range(3):
        make_final(wfinal_ref, final_ref, part)
    stores = [
        pltpu.make_async_copy(src, dst, store_sem.at[n])
        for n, (src, dst) in enumerate(((band_ref, band_hbm), (lift_ref, lift_hbm), (final_ref, final_hbm)))
    ]
    for copy in stores:
        copy.start()
    for out in third:
        out.wait_recv()
    for part in range(3):
        blocks_ref[part, 0:64] = above[part].reshape(64, width)
        blocks_ref[part, 64:192] = own[part].reshape(128, width)
        blocks_ref[part, 192:256] = below[part].reshape(64, width)
    for out, _ in first + second:
        out.wait_send()
    for out in third:
        out.wait_send()
    for copy in stores:
        copy.wait()


def exchange(latents, tile_slot, w_in, w_lift, w_final):
    rows, frames = lax.axis_size("rows"), lax.axis_size("frames")
    width = latents.shape[1]
    vmem, hbm = pl.BlockSpec(memory_space=pltpu.VMEM), pl.BlockSpec(memory_space=pltpu.HBM)
    weights = (w_in, w_lift.swapaxes(2, 3), w_final)
    made = [(768, 768), (1536, 768), (4, 768, 512)]
    dma = pltpu.SemaphoreType.DMA
    return pl.pallas_call(
        functools.partial(exchange_kernel, rows, frames),
        in_specs=[vmem, vmem, hbm, hbm, hbm],
        out_specs=[vmem, hbm, hbm, hbm],
        out_shape=[jax.ShapeDtypeStruct(shape, BF16) for shape in [(3, 256, width)] + made],
        scratch_shapes=[
            pltpu.VMEM((rows, 2 * frames, 2 * width), BF16),
            pltpu.VMEM((rows, 2 * frames, 2 * width), BF16),
            pltpu.VMEM((frames, 2 * rows, 2 * width), BF16),
            pltpu.VMEM((frames, 2 * rows, 2 * width), BF16),
            pltpu.VMEM((3, 2, 32, width), BF16),
            pltpu.VMEM((3, 2, 64, width), BF16),
            pltpu.VMEM((3, 2, 32, width), BF16),
        ]
        + [pltpu.VMEM(w.shape, BF16) for w in weights]
        + [pltpu.VMEM(shape, BF16) for shape in made]
        + [dma((3,)), dma((3,)), dma((rows,)), dma((rows,)), dma((frames,)), dma((frames,)), dma((8,)), dma((8,))],
        compiler_params=pltpu.CompilerParams(
            collective_id=0, has_side_effects=True, vmem_limit_bytes=40 * 1024 * 1024
        ),
        name="exchange",
    )(latents, tile_slot, *weights)


def shards(
    latents, tile_slot, w_in, b_in, gain_in, w_time, b_time, w_lift, b_lift, gain_lift, w_final, b_final
):
    blocks, band, wl, wf = exchange(latents, tile_slot, w_in, w_lift, w_final)
    return decode(blocks, band, wl, wf, b_in, gain_in, w_time, b_time, b_lift, gain_lift, b_final)


def solution(mesh):
    in_specs = (P(("rows", "frames"), None), P(("rows", "frames"))) + (P(),) * 10
    out_specs = P("frames", "rows", None)
    return jax.shard_map(shards, mesh=mesh, in_specs=in_specs, out_specs=out_specs, check_vma=False)
```

```python
import functools

import jax
import jax.numpy as jnp
from jax import lax
from jax.experimental import pallas as pl
from jax.experimental.pallas import tpu as pltpu
from jax.sharding import PartitionSpec as P

BF16, F32 = jnp.bfloat16, jnp.float32
XB = 32
SC = 8
VMEM_LIMIT = 60 * 1024 * 1024


def silu(n):
    half = 0.5 * n
    return half + half * jnp.tanh(half)


def pick(parts, tap, phase):
    if phase == 0:
        return parts[0] + parts[1] if tap == 0 else parts[2]
    return parts[0] if tap == 0 else parts[1] + parts[2]


def summed_taps(load, ty, tx, py, px):
    rows = [pick([load(dy, dx) for dy in range(3)], ty, py) for dx in range(3)]
    return pick(rows, tx, px)


def make_band(win_ref, band_ref):
    channels = win_ref.shape[-1]
    band_ref[...] = jnp.zeros_like(band_ref)
    for k in range(3):
        for dy in range(3):
            for dx in range(3):
                taps = win_ref[k, dy, dx]
                for pp in range(2):
                    row = 256 * k + 64 * dy + 16 * (dx + pp)
                    band_ref[row : row + 16, channels * pp : channels * (pp + 1)] = taps


def make_lift(wlift_ref, lift_ref, ty, tx):
    depth = wlift_ref.shape[-1]

    def part(lo, hi, py, px):
        return summed_taps(lambda dy, dx: wlift_ref[dy, dx, lo:hi, :].astype(F32), ty, tx, py, px)

    for px in range(2):
        tiles = [
            part(0, 128, 0, px),
            jnp.concatenate([part(128, 192, 0, px), part(128, 192, 1, px)], axis=0),
            part(0, 128, 1, px),
        ]
        for n, tile in enumerate(tiles):
            lane = 384 * px + 128 * n
            row = depth * (2 * ty + tx)
            lift_ref[row : row + depth, lane : lane + 128] = tile.T.astype(BF16)


def make_final(wfinal_ref, final_ref, part):
    rows = slice(64 * part, 64 * (part + 1))
    low = lax.broadcasted_iota(jnp.int32, (64, 128), 1) < 64
    pad = jnp.zeros((64, 32), F32)

    def load(dy, dx):
        return wfinal_ref[dy, dx, rows, :].astype(F32)

    for ty in range(2):
        for tx in range(2):
            for qy in range(2):
                q0, q1 = (jnp.concatenate([summed_taps(load, ty, tx, qy, qx), pad], axis=-1) for qx in range(2))
                r0, r1 = pltpu.roll(q0, 96, 1), pltpu.roll(q1, 64, 1)
                pairs = ((jnp.where(low, r1, r0), jnp.where(low, r0, r1)), (pltpu.roll(q0, 32, 1), q1))
                for xpar, tiles in enumerate(pairs):
                    px = tx if xpar else 1 - tx
                    for jpar in range(2):
                        py = ty if jpar else 1 - ty
                        slot = 384 * px + (256 * py + 64 * part if part < 2 else 128 + 64 * py)
                        for n, tile in enumerate(tiles):
                            lane = 256 * qy + 128 * n
                            final_ref[2 * jpar + xpar, slot : slot + 64, lane : lane + 128] = tile.astype(BF16)


def front(blocks_ref, band_ref, bin_ref, gin_ref, wtime_ref, btime_ref, grid_ref, dbl_ref, loads):
    row, frame = lax.axis_index("rows"), lax.axis_index("frames")
    top, bottom = row == 0, row == lax.axis_size("rows") - 1
    out_row = lax.broadcasted_iota(jnp.int32, (256, 256), 0)
    in_row = lax.broadcasted_iota(jnp.int32, (256, 256), 1)
    t, s, y = out_row // 128, (out_row // 8) % 16, out_row % 8
    wanted = jnp.where(
        y < 2,
        32 * t + 16 * y + s,
        jnp.where(y < 6, 64 + 64 * t + 16 * (y - 2) + s, 192 + 32 * t + 16 * (y - 6) + s),
    )
    inside = jnp.logical_and(
        jnp.logical_or(jnp.logical_not(top), y >= 2), jnp.logical_or(jnp.logical_not(bottom), y < 6)
    )
    chosen = jnp.logical_and(in_row == wanted, inside)
    zero_col = jnp.zeros((6, 1, 8, 128), F32)
    grid_ref[:, 0:1] = zero_col
    grid_ref[:, 17:18] = zero_col
    for part in range(3):
        select = jnp.where(jnp.logical_and(chosen, frame + part >= 2), 1.0, 0.0).astype(BF16)
        picked = jnp.dot(select, blocks_ref[part], preferred_element_type=F32)
        grid_ref[2 * part : 2 * part + 2, 1:17] = picked.reshape(2, 16, 8, 128)

    lane = lax.broadcasted_iota(jnp.int32, (1, 1, 1, 128), 3)
    sub = lax.broadcasted_iota(jnp.int32, (1, 1, 8, 1), 2)
    edge_col = jnp.zeros((1, 16, 384), BF16)
    for v in range(3):
        dbl_ref[v, 0:1] = edge_col
        dbl_ref[v, dbl_ref.shape[1] - 1 :] = edge_col

    loads[0].wait()
    loads[1].wait()
    b_in, g_in, b_time = (v[...].reshape(1, -1) for v in (bin_ref, gin_ref, btime_ref))

    def chunk(step, carry):
        s0 = step * SC
        cells = grid_ref[:, pl.ds(s0, SC + 2)]
        flat = cells.reshape(6 * (SC + 2), 8, 128)
        turned = [pltpu.roll(flat, 1, 1), flat, pltpu.roll(flat, 7, 1)]
        pieces = []
        for q in range(4):
            shift = (16 - 32 * q) % 128
            parts = []
            for d, lanes in enumerate((shift, shift + 64, shift)):
                moved = pltpu.roll(turned[d], lanes % 128, 2).reshape(6, SC + 2, 8, 128)
                own = moved[:, 1:-1]
                at = 64 * (d % 2)
                if q == 0:
                    own = jnp.where((lane >= at) & (lane < at + 16), moved[:, :-2], own)
                if q == 3:
                    own = jnp.where((lane >= at + 48) & (lane < at + 64), moved[:, 2:], own)
                parts.append(own)
            first = jnp.where(lane < 64, parts[0], parts[1])
            pieces.append(jnp.concatenate([first, parts[2]], axis=-1))
        patch = jnp.stack(pieces, axis=2).reshape(6, SC * 4 * 8, 256).astype(BF16)
        patch = jnp.concatenate([patch[k : k + 4] for k in range(3)], axis=-1)
        hidden = jnp.dot(patch.reshape(4 * SC * 32, 768), band_ref[...], preferred_element_type=F32)
        halves = []
        for pp in range(2):
            h = hidden[:, 384 * pp : 384 * (pp + 1)] + b_in
            mean = jnp.sum(h * h, axis=-1, keepdims=True) * (1.0 / 384)
            v = silu(h * lax.rsqrt(mean + 1e-6) * g_in)
            halves.append(v.reshape(4, SC * 4, 8, 384))
        feats = jnp.stack(halves, axis=2)
        t_in = lax.broadcasted_iota(jnp.int32, (4, 1, 1, 1, 1), 0)
        feats = jnp.where(t_in + 2 * frame >= 2, feats, 0.0)
        feats = feats.reshape(4, SC * 64, 384).astype(BF16)
        hist = jnp.concatenate([feats[k : k + 2] for k in range(3)], axis=-1)
        acc = jnp.dot(hist.reshape(2 * SC * 64, 1152), wtime_ref[...], preferred_element_type=F32)
        acc = acc + b_time
        acc = acc.reshape(2, SC * 8, 8, 768)
        for v in range(3):
            both = []
            for j in range(2):
                a0 = pltpu.roll(acc[0, :, :, 384 * j : 384 * (j + 1)], 7 - v, 1)
                a1 = pltpu.roll(acc[1, :, :, 384 * j : 384 * (j + 1)], 3 - v, 1)
                both.append(jnp.where(sub[0] < 4, a0, a1))
            full = jnp.concatenate(both, axis=1)
            group = lax.broadcasted_iota(jnp.int32, (1, 16, 1), 1) % 4
            if v == 0:
                full = jnp.where(jnp.logical_and(top, group == 0), 0.0, full)
            if v == 2:
                full = jnp.where(jnp.logical_and(bottom, group == 3), 0.0, full)
            dbl_ref[v, pl.ds(8 * s0 + 1, SC * 8)] = full.astype(BF16)
        return carry

    lax.fori_loop(0, 16 // SC, chunk, 0)


def back(step, dbl_ref, wl_ref, bl_ref, gl_ref, wf_ref, bf_ref, out_ref, rows_ref):
    row = lax.axis_index("rows")
    top, bottom = row == 0, row == lax.axis_size("rows") - 1
    width = dbl_ref.shape[1] - 2
    x0 = step * XB
    count = XB + 1
    lane = lax.broadcasted_iota(jnp.int32, (1, 1, 128), 2)
    low = lane < 64
    d_m, d_0, d_p = (dbl_ref[v, pl.ds(x0, XB + 2)] for v in range(3))
    group = lax.broadcasted_iota(jnp.int32, (1, 16, 1), 1) % 4
    col = lax.broadcasted_iota(jnp.int32, (count, 1, 1), 0) + (x0 - 1)

    def lift(upper, lower, drop):
        patch = jnp.concatenate([upper[:-1], upper[1:], lower[:-1], lower[1:]], axis=-1)
        acc = jnp.dot(patch.reshape(count * 16, -1), wl_ref[...], preferred_element_type=F32)
        acc = acc.reshape(count, 16, 768) + bl_ref[...]
        out = []
        for px in range(2):
            tiles = [acc[..., 384 * px + 128 * k : 384 * px + 128 * (k + 1)] for k in range(3)]
            sq = [v * v for v in tiles]
            s0 = jnp.sum(sq[0] + jnp.where(low, sq[1], 0.0), axis=-1, keepdims=True)
            s1 = jnp.sum(sq[2] + jnp.where(low, 0.0, sq[1]), axis=-1, keepdims=True)
            f0 = lax.rsqrt(s0 * (1.0 / 192) + 1e-6)
            f1 = lax.rsqrt(s1 * (1.0 / 192) + 1e-6)
            inside = (col >= 0) if px == 0 else (col < width - 1)
            for k, f in enumerate((f0, jnp.where(low, f0, f1), f1)):
                v = silu(tiles[k] * f * gl_ref[:, 384 * px + 128 * k : 384 * px + 128 * (k + 1)])
                keep = inside if drop[k] is None else jnp.logical_and(inside, jnp.logical_not(drop[k]))
                out.append(jnp.where(keep, v, 0.0).astype(BF16))
        return out

    above = jnp.logical_and(group == 0, top)
    below = jnp.logical_and(group == 3, bottom)
    s_m = lift(d_m, d_0, (above, jnp.logical_and(above, low), None))
    s_p = lift(d_0, d_p, (None, jnp.logical_and(below, jnp.logical_not(low)), below))
    s_e = []
    for px in range(2):
        s_e += [s_p[3 * px], jnp.where(low, s_p[3 * px + 1], s_m[3 * px + 1]), s_m[3 * px + 2]]

    def odd(tiles):
        return jnp.concatenate(tiles, axis=-1).reshape(count * 16, 768)

    def even(tiles):
        return jnp.concatenate([v[1:] for v in tiles[:3]] + [v[:-1] for v in tiles[3:]], axis=-1).reshape(XB * 16, 768)

    def mul(lhs, kind, lo, hi):
        return jnp.dot(lhs, wf_ref[kind, :, lo:hi], preferred_element_type=F32).reshape(-1, 16, hi - lo)

    e_o, e_e = mul(odd(s_e), 1, 0, 512), mul(even(s_e), 0, 0, 512)
    results = (
        (mul(odd(s_m), 3, 256, 512), mul(even(s_m), 2, 256, 512)),
        (e_o[..., :256], e_e[..., :256]),
        (e_o[..., 256:], e_e[..., 256:]),
        (mul(odd(s_p), 3, 0, 256), mul(even(s_p), 2, 0, 256)),
    )
    for a, (o, e) in enumerate(results):
        t0 = jnp.where(lane < 96, o[:-1, :, 128:], e[..., :128])
        t1 = e[..., 128:]
        t2 = jnp.where(lane < 32, e[..., :128], o[1:, :, :128])
        for k, t in enumerate((t0, t1, t2)):
            t = t + bf_ref[:, 128 * k : 128 * (k + 1)]
            for u in range(XB):
                rows_ref[3 * u + k, pl.ds(a, 16, stride=4), :] = t[u]
    for j in range(2):
        for t in range(2):
            base = 16 * (2 * j + t)
            for n in range(3 * XB):
                out_ref[2 * t + j, :, 128 * n : 128 * (n + 1)] = rows_ref[n, base : base + 16, :].astype(BF16)


def spread(half):
    wide, narrow = half[:, :128], half[:, 128:]
    return jnp.concatenate([wide, narrow, narrow, wide] * 2, axis=-1)


def decode_kernel(
    blocks_ref, band_hbm, bin_ref, gin_ref, wtime_hbm, btime_ref, lift_hbm, blift_ref, glift_ref, final_hbm, bfinal_ref,
    out_ref, grid_ref, dbl_ref, rows_ref, band_ref, wtime_ref, wl_ref, wf_ref, bl_ref, gl_ref, bf_ref, load_sem,
):
    step = pl.program_id(0)

    @pl.when(step == 0)
    def _():
        loads = [
            pltpu.make_async_copy(src, dst, load_sem.at[n])
            for n, (src, dst) in enumerate(
                ((band_hbm, band_ref), (wtime_hbm, wtime_ref), (lift_hbm, wl_ref), (final_hbm, wf_ref))
            )
        ]
        for copy in loads:
            copy.start()
        bl_ref[...] = spread(blift_ref[...].reshape(1, -1))
        gl_ref[...] = spread(glift_ref[...].reshape(1, -1))
        bf_ref[...] = jnp.concatenate([bfinal_ref[...].reshape(1, -1)] * 4, axis=-1)
        front(blocks_ref, band_ref, bin_ref, gin_ref, wtime_ref, btime_ref, grid_ref, dbl_ref, loads)
        loads[2].wait()
        loads[3].wait()

    back(step, dbl_ref, wl_ref, bl_ref, gl_ref, wf_ref, bf_ref, out_ref, rows_ref)


def decode(blocks, band, wl, wf, b_in, gain_in, w_time, b_time, b_lift, gain_lift, b_final):
    width = 128
    vmem, hbm = pl.BlockSpec(memory_space=pltpu.VMEM), pl.BlockSpec(memory_space=pltpu.HBM)
    w_time = w_time.reshape(-1, w_time.shape[-1])
    weights = (band, w_time, wl, wf)
    return pl.pallas_call(
        decode_kernel,
        grid=(width // XB,),
        in_specs=[vmem, hbm, vmem, vmem, hbm, vmem, hbm, vmem, vmem, hbm, vmem],
        out_specs=pl.BlockSpec((4, 16, XB * 384), lambda i: (0, 0, i)),
        out_shape=jax.ShapeDtypeStruct((4, 16, width * 384), BF16),
        scratch_shapes=[
            pltpu.VMEM((6, 18, 8, 128), F32),
            pltpu.VMEM((3, width + 2, 16, 384), BF16),
            pltpu.VMEM((XB * 3, 64, 128), F32),
        ]
        + [pltpu.VMEM(w.shape, BF16) for w in weights]
        + [pltpu.VMEM((1, 768), F32), pltpu.VMEM((1, 768), F32), pltpu.VMEM((1, 384), F32)]
        + [pltpu.SemaphoreType.DMA((4,))],
        compiler_params=pltpu.CompilerParams(vmem_limit_bytes=VMEM_LIMIT),
        name="decode",
    )(blocks, band, b_in, gain_in, w_time, b_time, wl, b_lift, gain_lift, wf, b_final)


def exchange_kernel(
    rows, frames,
    lat_ref, slot_ref, win_hbm, wlift_hbm, wfinal_hbm,
    blocks_ref, band_hbm, lift_hbm, final_hbm,
    send1, recv1, send2, recv2, above, own, below, win_ref, wlift_ref, wfinal_ref, band_ref, lift_ref, final_ref,
    load_sem, store_sem, send_sem1, recv_sem1, send_sem2, recv_sem2, send_sem3, recv_sem3,
):
    r, f = lax.axis_index("rows"), lax.axis_index("frames")
    loads = [
        pltpu.make_async_copy(src, dst, load_sem.at[n])
        for n, (src, dst) in enumerate(((win_hbm, win_ref), (wlift_hbm, wlift_ref), (wfinal_hbm, wfinal_ref)))
    ]
    for copy in loads:
        copy.start()

    def at(dr, df):
        return {"rows": lax.rem(r + dr + rows, rows), "frames": lax.rem(f + df + frames, frames)}

    near = [(dr, df) for df in range(3) for dr in (0, 1, -1) if (dr, df) != (0, 0)]
    far = [(dr, df) for dr, df in near if dr != 0 and df != 0]
    barrier = pltpu.get_barrier_semaphore()
    sources = [(k, 0) for k in range(1, rows)] + [(0, k) for k in range(1, frames)] + [(-dr, -df) for dr, df in far]
    for dr, df in sources:
        pl.semaphore_signal(barrier, inc=1, device_id=at(dr, df), device_id_type=pl.DeviceIdType.MESH)

    slots, width = lat_ref.shape
    across = jnp.broadcast_to(slot_ref[...].reshape(1, slots), (slots, slots))
    down = across.T
    index = lax.broadcasted_iota(jnp.int32, (slots, slots), 0)
    lane = lax.broadcasted_iota(jnp.int32, (slots, slots), 1)
    twin = jnp.logical_and(across // slots == down // slots, index < lane)
    rank = jnp.sum(jnp.where(twin, 1, 0), axis=0, keepdims=True)
    target = 2 * (across[:1] // slots) + rank
    total = 2 * rows * frames
    place = lax.broadcasted_iota(jnp.int32, (total, slots), 0) == target
    tags = (down % slots + 1).astype(F32).astype(BF16)
    tagged = jnp.concatenate([lat_ref[...], tags], axis=-1)
    packed = jnp.dot(jnp.where(place, 1.0, 0.0).astype(BF16), tagged, preferred_element_type=F32)
    send1[...] = packed.astype(BF16).reshape(send1.shape)
    recv1[r] = send1[r]
    pl.semaphore_wait(barrier, len(sources))

    def remote(src, dst, send, recv, dr, df):
        return pltpu.make_async_remote_copy(
            src_ref=src, dst_ref=dst, send_sem=send, recv_sem=recv,
            device_id=at(dr, df), device_id_type=pl.DeviceIdType.MESH,
        )

    first = []
    for k in range(1, rows):
        peer, source = lax.rem(r + k, rows), lax.rem(r - k + rows, rows)
        out = remote(send1.at[peer], recv1.at[r], send_sem1.at[k], recv_sem1.at[k], k, 0)
        out.start()
        first.append((out, remote(send1.at[peer], recv1.at[source], send_sem1.at[k], recv_sem1.at[k], k, 0)))
    loads[0].wait()
    make_band(win_ref, band_ref)
    loads[1].wait()
    make_lift(wlift_ref, lift_ref, 0, 0)
    for out, arrival in first:
        arrival.wait_recv()

    o = lax.broadcasted_iota(jnp.int32, (total, total), 0)
    i = lax.broadcasted_iota(jnp.int32, (total, total), 1)
    group = 2 * rows
    regroup = i == ((o // 2) % rows) * (2 * frames) + (o // group) * 2 + o % 2
    moved = jnp.dot(
        jnp.where(regroup, 1.0, 0.0).astype(BF16), recv1[...].reshape(total, 2 * width), preferred_element_type=F32
    )
    send2[...] = moved.astype(BF16).reshape(send2.shape)
    recv2[f] = send2[f]
    second = []
    for k in range(1, frames):
        peer, source = lax.rem(f + k, frames), lax.rem(f - k + frames, frames)
        out = remote(send2.at[peer], recv2.at[f], send_sem2.at[k], recv_sem2.at[k], 0, k)
        out.start()
        second.append((out, remote(send2.at[peer], recv2.at[source], send_sem2.at[k], recv_sem2.at[k], 0, k)))
    make_lift(wlift_ref, lift_ref, 0, 1)
    make_lift(wlift_ref, lift_ref, 1, 0)
    for out, arrival in second:
        arrival.wait_recv()

    arrived = recv2[...].reshape(total, 2 * width)
    want = lax.broadcasted_iota(jnp.int32, (total, slots), 1).astype(F32) + 1.0
    land = jnp.where(arrived[:, width:].astype(F32) == want, 1.0, 0.0).astype(BF16)
    canvas = lax.dot_general(land, arrived[:, :width], (((0,), (0,)), ((), ())), preferred_element_type=F32)
    own[2] = canvas.astype(BF16).reshape(2, 64, width)
    third = []
    for n, (dr, df) in enumerate(near):
        src, region = {
            0: (own.at[2], own),
            1: (own.at[2, :, pl.ds(32, 32)], above),
            -1: (own.at[2, :, pl.ds(0, 32)], below),
        }[dr]
        out = remote(src, region.at[2 - df], send_sem3.at[n], recv_sem3.at[n], dr, df)
        out.start()
        third.append(out)
    make_lift(wlift_ref, lift_ref, 1, 1)
    loads[2].wait()
    for part in range(3):
        make_final(wfinal_ref, final_ref, part)
    stores = [
        pltpu.make_async_copy(src, dst, store_sem.at[n])
        for n, (src, dst) in enumerate(((band_ref, band_hbm), (lift_ref, lift_hbm), (final_ref, final_hbm)))
    ]
    for copy in stores:
        copy.start()
    for out in third:
        out.wait_recv()
    for part in range(3):
        blocks_ref[part, 0:64] = above[part].reshape(64, width)
        blocks_ref[part, 64:192] = own[part].reshape(128, width)
        blocks_ref[part, 192:256] = below[part].reshape(64, width)
    for out, _ in first + second:
        out.wait_send()
    for out in third:
        out.wait_send()
    for copy in stores:
        copy.wait()


def exchange(latents, tile_slot, w_in, w_lift, w_final):
    rows, frames = lax.axis_size("rows"), lax.axis_size("frames")
    width = latents.shape[1]
    vmem, hbm = pl.BlockSpec(memory_space=pltpu.VMEM), pl.BlockSpec(memory_space=pltpu.HBM)
    weights = (w_in, w_lift.swapaxes(2, 3), w_final)
    made = [(768, 768), (1536, 768), (4, 768, 512)]
    dma = pltpu.SemaphoreType.DMA
    return pl.pallas_call(
        functools.partial(exchange_kernel, rows, frames),
        in_specs=[vmem, vmem, hbm, hbm, hbm],
        out_specs=[vmem, hbm, hbm, hbm],
        out_shape=[jax.ShapeDtypeStruct(shape, BF16) for shape in [(3, 256, width)] + made],
        scratch_shapes=[
            pltpu.VMEM((rows, 2 * frames, 2 * width), BF16),
            pltpu.VMEM((rows, 2 * frames, 2 * width), BF16),
            pltpu.VMEM((frames, 2 * rows, 2 * width), BF16),
            pltpu.VMEM((frames, 2 * rows, 2 * width), BF16),
            pltpu.VMEM((3, 2, 32, width), BF16),
            pltpu.VMEM((3, 2, 64, width), BF16),
            pltpu.VMEM((3, 2, 32, width), BF16),
        ]
        + [pltpu.VMEM(w.shape, BF16) for w in weights]
        + [pltpu.VMEM(shape, BF16) for shape in made]
        + [dma((3,)), dma((3,)), dma((rows,)), dma((rows,)), dma((frames,)), dma((frames,)), dma((8,)), dma((8,))],
        compiler_params=pltpu.CompilerParams(
            collective_id=0, has_side_effects=True, vmem_limit_bytes=VMEM_LIMIT
        ),
        name="exchange",
    )(latents, tile_slot, *weights)


def shards(
    latents, tile_slot, w_in, b_in, gain_in, w_time, b_time, w_lift, b_lift, gain_lift, w_final, b_final
):
    blocks, band, wl, wf = exchange(latents, tile_slot, w_in, w_lift, w_final)
    return decode(blocks, band, wl, wf, b_in, gain_in, w_time, b_time, b_lift, gain_lift, b_final)


def solution(mesh):
    in_specs = (P(("rows", "frames"), None), P(("rows", "frames"))) + (P(),) * 10
    out_specs = P("frames", "rows", None)
    return jax.shard_map(shards, mesh=mesh, in_specs=in_specs, out_specs=out_specs, check_vma=False)
```

```python
import functools

import jax
import jax.numpy as jnp
from jax import lax
from jax.experimental import pallas as pl
from jax.experimental.pallas import tpu as pltpu
from jax.sharding import PartitionSpec as P

BF16, F32 = jnp.bfloat16, jnp.float32
XB = 64
SUB = 32
SC = 8
VMEM_LIMIT = 60 * 1024 * 1024


def silu_of_half(half):
    return half + half * jnp.tanh(half)


def pick(parts, tap, phase):
    if phase == 0:
        return parts[0] + parts[1] if tap == 0 else parts[2]
    return parts[0] if tap == 0 else parts[1] + parts[2]


def summed_taps(load, ty, tx, py, px):
    rows = [pick([load(dy, dx) for dy in range(3)], ty, py) for dx in range(3)]
    return pick(rows, tx, px)


def make_band(win_ref, band_ref):
    channels = win_ref.shape[-1]
    band_ref[...] = jnp.zeros_like(band_ref)
    for k in range(3):
        for dy in range(3):
            for dx in range(3):
                taps = win_ref[k, dy, dx]
                for pp in range(2):
                    row = 256 * k + 64 * dy + 16 * (dx + pp)
                    band_ref[row : row + 16, channels * pp : channels * (pp + 1)] = taps


def make_lift(wlift_ref, lift_ref, ty, tx):
    depth = wlift_ref.shape[-1]

    def part(lo, hi, py, px):
        return summed_taps(lambda dy, dx: wlift_ref[dy, dx, lo:hi, :].astype(F32), ty, tx, py, px)

    for px in range(2):
        tiles = [
            part(0, 128, 0, px),
            jnp.concatenate([part(128, 192, 0, px), part(128, 192, 1, px)], axis=0),
            part(0, 128, 1, px),
        ]
        for n, tile in enumerate(tiles):
            lane = 384 * px + 128 * n
            row = depth * (2 * ty + tx)
            lift_ref[row : row + depth, lane : lane + 128] = tile.T.astype(BF16)


def make_final(wfinal_ref, final_ref, part):
    rows = slice(64 * part, 64 * (part + 1))
    low = lax.broadcasted_iota(jnp.int32, (64, 128), 1) < 64
    pad = jnp.zeros((64, 32), F32)

    def load(dy, dx):
        return wfinal_ref[dy, dx, rows, :].astype(F32)

    for ty in range(2):
        for tx in range(2):
            for qy in range(2):
                q0, q1 = (jnp.concatenate([summed_taps(load, ty, tx, qy, qx), pad], axis=-1) for qx in range(2))
                r0, r1 = pltpu.roll(q0, 96, 1), pltpu.roll(q1, 64, 1)
                pairs = ((jnp.where(low, r1, r0), jnp.where(low, r0, r1)), (pltpu.roll(q0, 32, 1), q1))
                for xpar, tiles in enumerate(pairs):
                    px = tx if xpar else 1 - tx
                    for jpar in range(2):
                        py = ty if jpar else 1 - ty
                        slot = 384 * px + (256 * py + 64 * part if part < 2 else 128 + 64 * py)
                        for n, tile in enumerate(tiles):
                            lane = 256 * qy + 128 * n
                            final_ref[2 * jpar + xpar, slot : slot + 64, lane : lane + 128] = tile.astype(BF16)


def front(block_refs, band_ref, bin_ref, gin_ref, wtime_ref, btime_ref, grid_ref, dbl_ref, loads):
    row, frame = lax.axis_index("rows"), lax.axis_index("frames")
    top, bottom = row == 0, row == lax.axis_size("rows") - 1
    out_row = lax.broadcasted_iota(jnp.int32, (256, 256), 0)
    in_row = lax.broadcasted_iota(jnp.int32, (256, 256), 1)
    t, s, y = out_row // 128, (out_row // 8) % 16, out_row % 8
    wanted = jnp.where(
        y < 2,
        32 * t + 16 * y + s,
        jnp.where(y < 6, 64 + 64 * t + 16 * (y - 2) + s, 192 + 32 * t + 16 * (y - 6) + s),
    )
    inside = jnp.logical_and(
        jnp.logical_or(jnp.logical_not(top), y >= 2), jnp.logical_or(jnp.logical_not(bottom), y < 6)
    )
    chosen = jnp.logical_and(in_row == wanted, inside)
    zero_col = jnp.zeros((6, 1, 8, 128), F32)
    grid_ref[:, 0:1] = zero_col
    grid_ref[:, 17:18] = zero_col
    for part in range(3):
        select = jnp.where(jnp.logical_and(chosen, frame + part >= 2), 1.0, 0.0).astype(BF16)
        cells = jnp.concatenate([ref[part].reshape(-1, 128) for ref in block_refs], axis=0)
        picked = jnp.dot(select, cells, preferred_element_type=F32)
        grid_ref[2 * part : 2 * part + 2, 1:17] = picked.reshape(2, 16, 8, 128)

    lane = lax.broadcasted_iota(jnp.int32, (1, 1, 1, 128), 3)
    sub = lax.broadcasted_iota(jnp.int32, (1, 1, 8, 1), 2)
    edge_col = jnp.zeros((3, 1, 32, 128), F32)
    dbl_ref[:, 0:1] = edge_col
    dbl_ref[:, dbl_ref.shape[1] - 1 :] = edge_col

    loads[0].wait()
    loads[1].wait()
    b_in, g_in, b_time = (v[...].reshape(1, -1) for v in (bin_ref, gin_ref, btime_ref))
    g_in = 0.5 * g_in

    def chunk(step, carry):
        s0 = step * SC
        cells = grid_ref[:, pl.ds(s0, SC + 2)]
        flat = cells.reshape(6 * (SC + 2), 8, 128)
        turned = [flat, pltpu.roll(flat, 7, 1), pltpu.roll(flat, 6, 1)]
        pieces = []
        for q in range(4):
            shift = (16 - 32 * q) % 128
            parts = []
            for d, lanes in enumerate((shift, shift + 64, shift)):
                moved = pltpu.roll(turned[d], lanes % 128, 2).reshape(6, SC + 2, 8, 128)
                own = moved[:, 1:-1]
                at = 64 * (d % 2)
                if q == 0:
                    own = jnp.where((lane >= at) & (lane < at + 16), moved[:, :-2], own)
                if q == 3:
                    own = jnp.where((lane >= at + 48) & (lane < at + 64), moved[:, 2:], own)
                parts.append(own)
            first = jnp.where(lane < 64, parts[0], parts[1])
            pieces.append(jnp.concatenate([first, parts[2]], axis=-1))
        patch = jnp.stack(pieces, axis=2).reshape(6, SC * 4 * 8, 256).astype(BF16)
        patch = jnp.concatenate([patch[k : k + 4] for k in range(3)], axis=-1)
        hidden = jnp.dot(patch.reshape(4 * SC * 32, 768), band_ref[...], preferred_element_type=F32)
        halves = []
        for pp in range(2):
            h = hidden[:, 384 * pp : 384 * (pp + 1)] + b_in
            mean = jnp.sum(h * h, axis=-1, keepdims=True) * (1.0 / 384)
            v = silu_of_half(h * lax.rsqrt(mean + 1e-6) * g_in)
            halves.append(v.reshape(4, SC * 4, 8, 384))
        feats = jnp.stack(halves, axis=2)
        feats = jnp.concatenate([jnp.where(frame > 0, feats[:2], 0.0), feats[2:]], axis=0)
        feats = feats.reshape(4, SC * 64, 384).astype(BF16)
        hist = jnp.concatenate([feats[k : k + 2] for k in range(3)], axis=-1)
        acc = jnp.dot(hist.reshape(2 * SC * 64, 1152), wtime_ref[...], preferred_element_type=F32)
        acc = acc + b_time
        acc = acc.reshape(2, SC * 8, 8, 768)
        for t in range(2):
            for j in range(2):
                for k in range(3):
                    lanes = acc[t, :, :, 384 * j + 128 * k : 384 * j + 128 * (k + 1)]
                    dbl_ref[k, pl.ds(8 * s0 + 1, SC * 8), pl.ds(2 * j + t, 8, stride=4), :] = lanes
        return carry

    lax.fori_loop(0, 16 // SC, chunk, 0)

    @pl.when(top)
    def _():
        dbl_ref[:, :, 0:4, :] = jnp.zeros((3, dbl_ref.shape[1], 4, 128), F32)

    @pl.when(bottom)
    def _():
        dbl_ref[:, :, 20:24, :] = jnp.zeros((3, dbl_ref.shape[1], 4, 128), F32)


def back(step, sub, dbl_ref, wl_ref, bl_ref, gl_ref, wf_ref, bf_ref, out_ref, rows_ref, sec_ref):
    row = lax.axis_index("rows")
    top, bottom = row == 0, row == lax.axis_size("rows") - 1
    width = dbl_ref.shape[1] - 2
    x0 = step * XB + sub
    count = SUB + 1
    lane = lax.broadcasted_iota(jnp.int32, (1, 1, 128), 2)
    low = lane < 64
    half = lax.broadcasted_iota(jnp.int32, (1, 8, 1), 1) < 4

    patch = []
    for ty in range(2):
        tiles = [dbl_ref[k, pl.ds(x0, count + 1), 4 * ty : 4 * ty + 24, :] for k in range(3)]
        patch += [v[tx : tx + count].reshape(count * 24, 128).astype(BF16) for tx in range(2) for v in tiles]
    acc = jnp.dot(jnp.concatenate(patch, axis=-1), wl_ref[...], preferred_element_type=F32)
    acc = acc.reshape(count, 24, 768) + bl_ref[...]
    first_rows = lax.broadcasted_iota(jnp.int32, (1, 8, 1), 1) < 4
    above, below = jnp.logical_and(first_rows, top), jnp.logical_and(first_rows, bottom)

    def keep(n, v):
        px, k = n // 3, n % 3
        for g in range(3):
            part = v[:, 8 * g : 8 * (g + 1)]
            if g == 0 and k < 2:
                part = jnp.where(above if k == 0 else jnp.logical_and(above, low), 0.0, part)
            if g == 2 and k > 0:
                part = jnp.where(below if k == 2 else jnp.logical_and(below, jnp.logical_not(low)), 0.0, part)
            rows = slice(16 + 8 * g, 24 + 8 * g)
            if px == 0:
                sec_ref[sub // SUB, n, 0:1, rows, :] = jnp.where(x0 == 0, 0.0, part[0:1])
                sec_ref[sub // SUB, n, 1:count, rows, :] = part[1:]
            else:
                sec_ref[sub // SUB, n, 0 : count - 1, rows, :] = part[:-1]
                sec_ref[sub // SUB, n, count - 1 : count, rows, :] = jnp.where(x0 == width - SUB, 0.0, part[-1:])

    for px in range(2):
        tiles = [acc[..., 384 * px + 128 * k : 384 * px + 128 * (k + 1)] for k in range(3)]
        sq = [v * v for v in tiles]
        s0 = jnp.sum(sq[0] + jnp.where(low, sq[1], 0.0), axis=-1, keepdims=True)
        s1 = jnp.sum(sq[2] + jnp.where(low, 0.0, sq[1]), axis=-1, keepdims=True)
        f0 = lax.rsqrt(s0 * (1.0 / 192) + 1e-6)
        f1 = lax.rsqrt(s1 * (1.0 / 192) + 1e-6)
        for k, f in enumerate((f0, jnp.where(low, f0, f1), f1)):
            v = silu_of_half(tiles[k] * f * gl_ref[:, 384 * px + 128 * k : 384 * px + 128 * (k + 1)])
            keep(3 * px + k, v)

    def window(k, first):
        out = []
        for h in range(2):
            lo = sec_ref[sub // SUB, k, :, pl.ds(16 + 4 * first + 2 * h, 8, stride=4), :]
            hi = sec_ref[sub // SUB, k, :, pl.ds(4 * first + 2 * h + 1, 8, stride=4), :]
            out.append(jnp.where(half, lo, hi))
        return jnp.concatenate(out, axis=1).astype(BF16)

    s_m = [window(k, 0) for k in range(6)]
    s_p = [window(k, 1) for k in range(6)]
    s_e = []
    for px in range(2):
        s_e += [s_p[3 * px], jnp.where(low, s_p[3 * px + 1], s_m[3 * px + 1]), s_m[3 * px + 2]]

    def odd(tiles):
        return jnp.concatenate(tiles, axis=-1).reshape(count * 16, 768)

    def even(tiles):
        return jnp.concatenate([v[1:] for v in tiles[:3]] + [v[:-1] for v in tiles[3:]], axis=-1).reshape(SUB * 16, 768)

    def mul(lhs, kind, lo, hi):
        return jnp.dot(lhs, wf_ref[kind, :, lo:hi], preferred_element_type=F32).reshape(-1, 16, hi - lo)

    e_o, e_e = mul(odd(s_e), 1, 0, 512), mul(even(s_e), 0, 0, 512)
    results = (
        (mul(odd(s_m), 3, 256, 512), mul(even(s_m), 2, 256, 512)),
        (e_o[..., :256], e_e[..., :256]),
        (e_o[..., 256:], e_e[..., 256:]),
        (mul(odd(s_p), 3, 0, 256), mul(even(s_p), 2, 0, 256)),
    )
    for a, (o, e) in enumerate(results):
        t0 = jnp.where(lane < 96, o[:-1, :, 128:], e[..., :128])
        t1 = e[..., 128:]
        t2 = jnp.where(lane < 32, e[..., :128], o[1:, :, :128])
        for k, t in enumerate((t0, t1, t2)):
            t = t + bf_ref[:, 128 * k : 128 * (k + 1)]
            for u in range(SUB):
                rows_ref[3 * (sub + u) + k, pl.ds(a, 16, stride=4), :] = t[u]
    for j in range(2):
        for t in range(2):
            base = 16 * (2 * j + t)
            for n in range(3 * sub, 3 * (sub + SUB)):
                out_ref[2 * t + j, :, 128 * n : 128 * (n + 1)] = rows_ref[n, base : base + 16, :].astype(BF16)


def spread(half):
    wide, narrow = half[:, :128], half[:, 128:]
    return jnp.concatenate([wide, narrow, narrow, wide] * 2, axis=-1)


def decode_kernel(
    above_ref, own_ref, below_ref, band_hbm, bin_ref, gin_ref, wtime_hbm, btime_ref, lift_hbm, blift_ref, glift_ref, final_hbm, bfinal_ref,
    out_ref, grid_ref, dbl_ref, rows_ref, sec_ref, band_ref, wtime_ref, wl_ref, wf_ref, bl_ref, gl_ref, bf_ref, load_sem,
):
    step = pl.program_id(0)

    @pl.when(step == 0)
    def _():
        loads = [
            pltpu.make_async_copy(src, dst, load_sem.at[n])
            for n, (src, dst) in enumerate(
                ((band_hbm, band_ref), (wtime_hbm, wtime_ref), (lift_hbm, wl_ref), (final_hbm, wf_ref))
            )
        ]
        for copy in loads:
            copy.start()
        bl_ref[...] = spread(blift_ref[...].reshape(1, -1))
        gl_ref[...] = 0.5 * spread(glift_ref[...].reshape(1, -1))
        bf_ref[...] = jnp.concatenate([bfinal_ref[...].reshape(1, -1)] * 4, axis=-1)
        front((above_ref, own_ref, below_ref), band_ref, bin_ref, gin_ref, wtime_ref, btime_ref, grid_ref, dbl_ref, loads)
        loads[2].wait()
        loads[3].wait()

    for sub in range(0, XB, SUB):
        back(step, sub, dbl_ref, wl_ref, bl_ref, gl_ref, wf_ref, bf_ref, out_ref, rows_ref, sec_ref)


def decode(above, own, below, band, wl, wf, b_in, gain_in, w_time, b_time, b_lift, gain_lift, b_final):
    width = 128
    vmem, hbm = pl.BlockSpec(memory_space=pltpu.VMEM), pl.BlockSpec(memory_space=pltpu.HBM)
    w_time = w_time.reshape(-1, w_time.shape[-1])
    weights = (band, w_time, wl, wf)
    return pl.pallas_call(
        decode_kernel,
        grid=(width // XB,),
        in_specs=[vmem, vmem, vmem, hbm, vmem, vmem, hbm, vmem, hbm, vmem, vmem, hbm, vmem],
        out_specs=pl.BlockSpec((4, 16, XB * 384), lambda i: (0, 0, i)),
        out_shape=jax.ShapeDtypeStruct((4, 16, width * 384), BF16),
        scratch_shapes=[
            pltpu.VMEM((6, 18, 8, 128), F32),
            pltpu.VMEM((3, width + 2, 32, 128), F32),
            pltpu.VMEM((XB * 3, 64, 128), F32),
            pltpu.VMEM((XB // SUB, 6, SUB + 1, 56, 128), F32),
        ]
        + [pltpu.VMEM(w.shape, BF16) for w in weights]
        + [pltpu.VMEM((1, 768), F32), pltpu.VMEM((1, 768), F32), pltpu.VMEM((1, 384), F32)]
        + [pltpu.SemaphoreType.DMA((4,))],
        compiler_params=pltpu.CompilerParams(vmem_limit_bytes=VMEM_LIMIT),
        name="decode",
    )(above, own, below, band, b_in, gain_in, w_time, b_time, wl, b_lift, gain_lift, wf, b_final)


def far_first(count):
    return sorted(range(1, count), key=lambda k: -min(k, count - k))


def exchange_kernel(
    rows, frames,
    lat_hbm, slot_hbm, win_hbm, wlift_hbm, wfinal_hbm,
    above, own, below, band_hbm, lift_hbm, final_hbm,
    lat_ref, slot_ref, send1, recv1, send2, recv2, block, win_ref, wlift_ref, wfinal_ref, band_ref, lift_ref, final_ref,
    load_sem, store_sem, send_sem1, recv_sem1, send_sem2, recv_sem2, send_sem3, recv_sem3,
):
    r, f = lax.axis_index("rows"), lax.axis_index("frames")
    loads = [
        pltpu.make_async_copy(src, dst, load_sem.at[n])
        for n, (src, dst) in enumerate(
            (
                (win_hbm, win_ref), (wlift_hbm, wlift_ref), (wfinal_hbm, wfinal_ref),
                (lat_hbm, lat_ref), (slot_hbm, slot_ref),
            )
        )
    ]
    loads[4].start()
    loads[3].start()

    def at(dr, df):
        return {"rows": lax.rem(r + dr + rows, rows), "frames": lax.rem(f + df + frames, frames)}

    near = [(dr, df) for df in range(3) for dr in (0, 1, -1) if (dr, df) != (0, 0)]
    far = [(dr, df) for dr, df in near if dr != 0 and df != 0]
    barrier = pltpu.get_barrier_semaphore()
    sources = [(k, 0) for k in range(1, rows)] + [(0, k) for k in range(1, frames)] + [(-dr, -df) for dr, df in far]
    for dr, df in sources:
        pl.semaphore_signal(barrier, inc=1, device_id=at(dr, df), device_id_type=pl.DeviceIdType.MESH)

    for copy in loads[:3]:
        copy.start()
    loads[4].wait()
    loads[3].wait()

    slots, width = lat_ref.shape
    across = jnp.broadcast_to(slot_ref[...].reshape(1, slots), (slots, slots))
    down = across.T
    index = lax.broadcasted_iota(jnp.int32, (slots, slots), 0)
    lane = lax.broadcasted_iota(jnp.int32, (slots, slots), 1)
    twin = jnp.logical_and(across // slots == down // slots, index < lane)
    rank = jnp.sum(jnp.where(twin, 1, 0), axis=0, keepdims=True)
    target = 2 * (across[:1] // slots) + rank
    total = 2 * rows * frames
    place = lax.broadcasted_iota(jnp.int32, (total, slots), 0) == target
    tags = (down % slots + 1).astype(F32).astype(BF16)
    tagged = jnp.concatenate([lat_ref[...], tags], axis=-1)
    packed = jnp.dot(jnp.where(place, 1.0, 0.0).astype(BF16), tagged, preferred_element_type=F32)
    send1[...] = packed.astype(BF16).reshape(send1.shape)
    recv1[r] = send1[r]
    pl.semaphore_wait(barrier, len(sources))

    def remote(src, dst, send, recv, dr, df):
        return pltpu.make_async_remote_copy(
            src_ref=src, dst_ref=dst, send_sem=send, recv_sem=recv,
            device_id=at(dr, df), device_id_type=pl.DeviceIdType.MESH,
        )

    first = []
    for k in far_first(rows):
        peer, source = lax.rem(r + k, rows), lax.rem(r - k + rows, rows)
        out = remote(send1.at[peer], recv1.at[r], send_sem1.at[k], recv_sem1.at[k], k, 0)
        out.start()
        first.append((out, remote(send1.at[peer], recv1.at[source], send_sem1.at[k], recv_sem1.at[k], k, 0)))
    loads[0].wait()
    make_band(win_ref, band_ref)
    loads[1].wait()
    make_lift(wlift_ref, lift_ref, 0, 0)
    for out, arrival in first:
        arrival.wait_recv()

    o = lax.broadcasted_iota(jnp.int32, (total, total), 0)
    i = lax.broadcasted_iota(jnp.int32, (total, total), 1)
    group = 2 * rows
    regroup = i == ((o // 2) % rows) * (2 * frames) + (o // group) * 2 + o % 2
    moved = jnp.dot(
        jnp.where(regroup, 1.0, 0.0).astype(BF16), recv1[...].reshape(total, 2 * width), preferred_element_type=F32
    )
    send2[...] = moved.astype(BF16).reshape(send2.shape)
    recv2[f] = send2[f]
    second = []
    for k in far_first(frames):
        peer, source = lax.rem(f + k, frames), lax.rem(f - k + frames, frames)
        out = remote(send2.at[peer], recv2.at[f], send_sem2.at[k], recv_sem2.at[k], 0, k)
        out.start()
        second.append((out, remote(send2.at[peer], recv2.at[source], send_sem2.at[k], recv_sem2.at[k], 0, k)))
    make_lift(wlift_ref, lift_ref, 0, 1)
    make_lift(wlift_ref, lift_ref, 1, 0)
    for out, arrival in second:
        arrival.wait_recv()

    arrived = recv2[...].reshape(total, 2 * width)
    want = lax.broadcasted_iota(jnp.int32, (total, slots), 1).astype(F32) + 1.0
    land = jnp.where(arrived[:, width:].astype(F32) == want, 1.0, 0.0).astype(BF16)
    canvas = lax.dot_general(land, arrived[:, :width], (((0,), (0,)), ((), ())), preferred_element_type=F32)
    block[...] = canvas.astype(BF16).reshape(2, 64, width)
    third = []
    for n, (dr, df) in enumerate(near):
        src, region = {
            0: (block, own),
            1: (block.at[:, pl.ds(32, 32)], above),
            -1: (block.at[:, pl.ds(0, 32)], below),
        }[dr]
        out = remote(src, region.at[2 - df], send_sem3.at[n], recv_sem3.at[n], dr, df)
        out.start()
        third.append(out)
    keep = pltpu.make_async_copy(block, own.at[2], load_sem.at[5])
    keep.start()
    make_lift(wlift_ref, lift_ref, 1, 1)
    loads[2].wait()
    for part in range(3):
        make_final(wfinal_ref, final_ref, part)
    stores = [
        pltpu.make_async_copy(src, dst, store_sem.at[n])
        for n, (src, dst) in enumerate(((band_ref, band_hbm), (lift_ref, lift_hbm), (final_ref, final_hbm)))
    ]
    for copy in stores:
        copy.start()
    for out in third:
        out.wait_recv()
    keep.wait()
    for out, _ in first + second:
        out.wait_send()
    for out in third:
        out.wait_send()
    for copy in stores:
        copy.wait()


def exchange(latents, tile_slot, w_in, w_lift, w_final):
    rows, frames = lax.axis_size("rows"), lax.axis_size("frames")
    width = latents.shape[1]
    hbm = pl.BlockSpec(memory_space=pltpu.HBM)
    weights = (w_in, w_lift.swapaxes(2, 3), w_final)
    made = [(768, 768), (1536, 768), (4, 768, 512)]
    blocks = [(3, 2, 32, width), (3, 2, 64, width), (3, 2, 32, width)]
    dma = pltpu.SemaphoreType.DMA
    return pl.pallas_call(
        functools.partial(exchange_kernel, rows, frames),
        in_specs=[hbm] * 5,
        out_specs=[hbm] * 6,
        out_shape=[jax.ShapeDtypeStruct(shape, BF16) for shape in blocks + made],
        scratch_shapes=[
            pltpu.VMEM(latents.shape, BF16),
            pltpu.VMEM(tile_slot.shape, jnp.int32),
            pltpu.VMEM((rows, 2 * frames, 2 * width), BF16),
            pltpu.VMEM((rows, 2 * frames, 2 * width), BF16),
            pltpu.VMEM((frames, 2 * rows, 2 * width), BF16),
            pltpu.VMEM((frames, 2 * rows, 2 * width), BF16),
            pltpu.VMEM((2, 64, width), BF16),
        ]
        + [pltpu.VMEM(w.shape, BF16) for w in weights]
        + [pltpu.VMEM(shape, BF16) for shape in made]
        + [dma((6,)), dma((3,)), dma((rows,)), dma((rows,)), dma((frames,)), dma((frames,)), dma((8,)), dma((8,))],
        compiler_params=pltpu.CompilerParams(
            collective_id=0, has_side_effects=True, vmem_limit_bytes=VMEM_LIMIT
        ),
        name="exchange",
    )(latents, tile_slot, *weights)


def shards(
    latents, tile_slot, w_in, b_in, gain_in, w_time, b_time, w_lift, b_lift, gain_lift, w_final, b_final
):
    above, own, below, band, wl, wf = exchange(latents, tile_slot, w_in, w_lift, w_final)
    return decode(above, own, below, band, wl, wf, b_in, gain_in, w_time, b_time, b_lift, gain_lift, b_final)


def solution(mesh):
    in_specs = (P(("rows", "frames"), None), P(("rows", "frames"))) + (P(),) * 10
    out_specs = P("frames", "rows", None)
    return jax.shard_map(shards, mesh=mesh, in_specs=in_specs, out_specs=out_specs, check_vma=False)
```

```python
import functools

import jax
import jax.numpy as jnp
from jax import lax
from jax.experimental import pallas as pl
from jax.experimental.pallas import tpu as pltpu
from jax.sharding import PartitionSpec as P

BF16, F32 = jnp.bfloat16, jnp.float32
XB = 64
NCH = 3
SUB = 32
SC = 8
VMEM_LIMIT = 60 * 1024 * 1024


def silu_of_half(half):
    return half + half * jnp.tanh(half)


def pick(parts, tap, phase):
    if phase == 0:
        return parts[0] + parts[1] if tap == 0 else parts[2]
    return parts[0] if tap == 0 else parts[1] + parts[2]


def summed_taps(load, ty, tx, py, px):
    rows = [pick([load(dy, dx) for dy in range(3)], ty, py) for dx in range(3)]
    return pick(rows, tx, px)


def make_band(win_ref, band_ref):
    channels = win_ref.shape[-1]
    band_ref[...] = jnp.zeros_like(band_ref)
    for k in range(3):
        for dy in range(3):
            for dx in range(3):
                taps = win_ref[k, dy, dx]
                for pp in range(2):
                    row = 256 * k + 64 * dy + 16 * (dx + pp)
                    band_ref[row : row + 16, channels * pp : channels * (pp + 1)] = taps


def make_lift(wlift_ref, lift_ref, ty, tx):
    depth = wlift_ref.shape[-1]

    def part(lo, hi, py, px):
        return summed_taps(lambda dy, dx: wlift_ref[dy, dx, lo:hi, :].astype(F32), ty, tx, py, px)

    for px in range(2):
        tiles = [
            part(0, 128, 0, px),
            jnp.concatenate([part(128, 192, 0, px), part(128, 192, 1, px)], axis=0),
            part(0, 128, 1, px),
        ]
        for n, tile in enumerate(tiles):
            lane = 384 * px + 128 * n
            row = depth * (2 * ty + tx)
            lift_ref[row : row + depth, lane : lane + 128] = tile.T.astype(BF16)


def make_final(wfinal_ref, final_ref, part):
    rows = slice(64 * part, 64 * (part + 1))
    low = lax.broadcasted_iota(jnp.int32, (64, 128), 1) < 64
    pad = jnp.zeros((64, 32), F32)

    def load(dy, dx):
        return wfinal_ref[dy, dx, rows, :].astype(F32)

    for ty in range(2):
        for tx in range(2):
            for qy in range(2):
                q0, q1 = (jnp.concatenate([summed_taps(load, ty, tx, qy, qx), pad], axis=-1) for qx in range(2))
                r0, r1 = pltpu.roll(q0, 96, 1), pltpu.roll(q1, 64, 1)
                pairs = ((jnp.where(low, r1, r0), jnp.where(low, r0, r1)), (pltpu.roll(q0, 32, 1), q1))
                for xpar, tiles in enumerate(pairs):
                    px = tx if xpar else 1 - tx
                    for jpar in range(2):
                        py = ty if jpar else 1 - ty
                        slot = 384 * px + (256 * py + 64 * part if part < 2 else 128 + 64 * py)
                        for n, tile in enumerate(tiles):
                            lane = 256 * qy + 128 * n
                            final_ref[2 * jpar + xpar, slot : slot + 64, lane : lane + 128] = tile.astype(BF16)


def weave(*lists):
    order = sorted(
        ((n + 0.5) / len(steps), which, n) for which, steps in enumerate(lists) for n in range(len(steps))
    )
    for _, which, n in order:
        lists[which][n]()


def front(block_refs, band_ref, bin_ref, gin_ref, wtime_ref, btime_ref, grid_ref, dbl_ref, loads):
    row, frame = lax.axis_index("rows"), lax.axis_index("frames")
    top, bottom = row == 0, row == lax.axis_size("rows") - 1
    out_row = lax.broadcasted_iota(jnp.int32, (256, 256), 0)
    in_row = lax.broadcasted_iota(jnp.int32, (256, 256), 1)
    t, s, y = out_row // 128, (out_row // 8) % 16, out_row % 8
    wanted = jnp.where(
        y < 2,
        32 * t + 16 * y + s,
        jnp.where(y < 6, 64 + 64 * t + 16 * (y - 2) + s, 192 + 32 * t + 16 * (y - 6) + s),
    )
    inside = jnp.logical_and(
        jnp.logical_or(jnp.logical_not(top), y >= 2), jnp.logical_or(jnp.logical_not(bottom), y < 6)
    )
    chosen = jnp.logical_and(in_row == wanted, inside)
    zero_col = jnp.zeros((6, 1, 8, 128), F32)
    grid_ref[:, 0:1] = zero_col
    grid_ref[:, 17:18] = zero_col
    for part in range(3):
        select = jnp.where(jnp.logical_and(chosen, frame + part >= 2), 1.0, 0.0).astype(BF16)
        cells = jnp.concatenate([ref[part].reshape(-1, 128) for ref in block_refs], axis=0)
        picked = jnp.dot(select, cells, preferred_element_type=F32)
        grid_ref[2 * part : 2 * part + 2, 1:17] = picked.reshape(2, 16, 8, 128)

    lane = lax.broadcasted_iota(jnp.int32, (1, 1, 1, 128), 3)
    sub = lax.broadcasted_iota(jnp.int32, (1, 1, 8, 1), 2)
    edge_col = jnp.zeros((3, 1, 32, 128), F32)
    dbl_ref[:, 0:1] = edge_col
    dbl_ref[:, dbl_ref.shape[1] - 1 :] = edge_col

    loads[0].wait()
    loads[1].wait()
    b_in, g_in, b_time = (v[...].reshape(1, -1) for v in (bin_ref, gin_ref, btime_ref))
    g_in = 0.5 * g_in

    def chunk(s0):
        pieces, hidden, feats, hist = [], [], [], []

        def build(q):
            flat = grid_ref[:, s0 : s0 + SC + 2].reshape(6 * (SC + 2), 8, 128)
            turned = [flat, pltpu.roll(flat, 7, 1), pltpu.roll(flat, 6, 1)]
            shift = (16 - 32 * q) % 128
            parts = []
            for d, lanes in enumerate((shift, shift + 64, shift)):
                moved = pltpu.roll(turned[d], lanes % 128, 2).reshape(6, SC + 2, 8, 128)
                own = moved[:, 1:-1]
                at = 64 * (d % 2)
                if q == 0:
                    own = jnp.where((lane >= at) & (lane < at + 16), moved[:, :-2], own)
                if q == 3:
                    own = jnp.where((lane >= at + 48) & (lane < at + 64), moved[:, 2:], own)
                parts.append(own)
            first = jnp.where(lane < 64, parts[0], parts[1])
            pieces.append(jnp.concatenate([first, parts[2]], axis=-1))

        def gather():
            patch = jnp.stack(pieces, axis=2).reshape(6, SC * 4 * 8, 256).astype(BF16)
            patch = jnp.concatenate([patch[k : k + 4] for k in range(3)], axis=-1)
            pieces.append(patch.reshape(4 * SC * 32, 768))

        def expand(n):
            out = jnp.dot(pieces[-1], band_ref[:, 256 * n : 256 * (n + 1)], preferred_element_type=F32)
            hidden.append(out.reshape(4, SC * 32, 256))

        def norm(t):
            tiles = []
            for pp in range(2):
                h = []
                for k in range(3):
                    n = 3 * pp + k
                    lanes = slice(128 * (n % 2), 128 * (n % 2) + 128)
                    h.append(hidden[n // 2][t][:, lanes] + b_in[:, 128 * k : 128 * (k + 1)])
                mean = jnp.sum(h[0] * h[0] + h[1] * h[1] + h[2] * h[2], axis=-1, keepdims=True) * (1.0 / 384)
                factor = lax.rsqrt(mean + 1e-6)
                tiles.append([silu_of_half(h[k] * factor * g_in[:, 128 * k : 128 * (k + 1)]) for k in range(3)])
            merged = []
            for k in range(3):
                v = jnp.stack([tiles[pp][k].reshape(SC * 4, 8, 128) for pp in range(2)], axis=1)
                if t < 2:
                    v = jnp.where(frame > 0, v, 0.0)
                merged.append(v.reshape(SC * 64, 128).astype(BF16))
            feats.append(merged)

        def align():
            rows = [jnp.concatenate([v for k in range(3) for v in feats[t + k]], axis=-1) for t in range(2)]
            hist.append(jnp.concatenate(rows, axis=0))

        def double(n):
            acc = jnp.dot(hist[0], wtime_ref[:, 256 * n : 256 * (n + 1)], preferred_element_type=F32)
            acc = (acc + b_time[:, 256 * n : 256 * (n + 1)]).reshape(2, SC * 8, 8, 256)
            for i in range(2):
                j, k = (2 * n + i) // 3, (2 * n + i) % 3
                for t in range(2):
                    lanes = acc[t, :, :, 128 * i : 128 * (i + 1)]
                    dbl_ref[k, 8 * s0 + 1 : 8 * (s0 + SC) + 1, pl.ds(2 * j + t, 8, stride=4), :] = lanes

        return (
            [functools.partial(build, q) for q in range(4)] + [gather] + [functools.partial(expand, n) for n in range(3)],
            [functools.partial(norm, t) for t in range(4)],
            [align] + [functools.partial(double, n) for n in range(3)],
        )

    chunks = [chunk(s0) for s0 in range(0, 16, SC)]
    for turn in range(len(chunks) + 2):
        weave(*(chunks[turn - n][n] for n in range(3) if 0 <= turn - n < len(chunks)))

    @pl.when(top)
    def _():
        dbl_ref[:, :, 0:4, :] = jnp.zeros((3, dbl_ref.shape[1], 4, 128), F32)

    @pl.when(bottom)
    def _():
        dbl_ref[:, :, 20:24, :] = jnp.zeros((3, dbl_ref.shape[1], 4, 128), F32)


class Columns:
    def __init__(self, step, sub, dbl_ref, wl_ref, bl_ref, gl_ref, wf_ref, bf_ref, out_ref, rows_ref, sec_ref):
        row = lax.axis_index("rows")
        self.top, self.bottom = row == 0, row == lax.axis_size("rows") - 1
        self.width = dbl_ref.shape[1] - 2
        self.x0, self.sub, self.count = step * XB + sub, sub, SUB + 1
        self.low = lax.broadcasted_iota(jnp.int32, (1, 1, 128), 2) < 64
        self.lane = lax.broadcasted_iota(jnp.int32, (1, 1, 128), 2)
        self.half = lax.broadcasted_iota(jnp.int32, (1, 8, 1), 1) < 4
        self.dbl_ref, self.wl_ref, self.bl_ref, self.gl_ref = dbl_ref, wl_ref, bl_ref, gl_ref
        self.wf_ref, self.bf_ref, self.out_ref, self.rows_ref = wf_ref, bf_ref, out_ref, rows_ref
        self.sec_ref = sec_ref.at[sub // SUB]
        self.acc, self.results, self.s_m, self.s_p, self.s_e = {}, {}, [], [], []

    def load(self):
        patch = []
        for ty in range(2):
            tiles = [self.dbl_ref[k, pl.ds(self.x0, self.count + 1), 4 * ty : 4 * ty + 24, :] for k in range(3)]
            patch += [
                v[tx : tx + self.count].reshape(self.count * 24, 128).astype(BF16) for tx in range(2) for v in tiles
            ]
        self.patch = jnp.concatenate(patch, axis=-1)

    def lift_steps(self):
        def part(n):
            w = self.wl_ref[:, 256 * n : 256 * (n + 1)]
            acc = jnp.dot(self.patch, w, preferred_element_type=F32)
            self.acc[n] = acc.reshape(self.count, 24, 256)

        return [self.load] + [functools.partial(part, n) for n in range(3)]

    def keep(self, n, lo, hi, v):
        px, k = n // 3, n % 3
        first_rows = lax.broadcasted_iota(jnp.int32, (1, 8, 1), 1) < 4
        above, below = jnp.logical_and(first_rows, self.top), jnp.logical_and(first_rows, self.bottom)
        for g in range(3):
            part = v[:, 8 * g : 8 * (g + 1)]
            if g == 0 and k < 2:
                part = jnp.where(above if k == 0 else jnp.logical_and(above, self.low), 0.0, part)
            if g == 2 and k > 0:
                part = jnp.where(below if k == 2 else jnp.logical_and(below, jnp.logical_not(self.low)), 0.0, part)
            rows = slice(16 + 8 * g, 24 + 8 * g)
            if px == 0 and lo == 0:
                self.sec_ref[n, 0:1, rows, :] = jnp.where(self.x0 == 0, 0.0, part[0:1])
                self.sec_ref[n, 1:hi, rows, :] = part[1:]
            elif px == 1 and hi == self.count:
                self.sec_ref[n, lo : hi - 1, rows, :] = part[:-1]
                self.sec_ref[n, hi - 1 : hi, rows, :] = jnp.where(self.x0 == self.width - SUB, 0.0, part[-1:])
            else:
                self.sec_ref[n, lo:hi, rows, :] = part

    def norm_steps(self):
        def part(lo, hi, px):
            tiles = []
            for k in range(3):
                n = 3 * px + k
                lanes = slice(128 * (n % 2), 128 * (n % 2) + 128)
                tiles.append(self.acc[n // 2][lo:hi, :, lanes] + self.bl_ref[:, 128 * n : 128 * (n + 1)])
            sq = [v * v for v in tiles]
            s0 = jnp.sum(sq[0] + jnp.where(self.low, sq[1], 0.0), axis=-1, keepdims=True)
            s1 = jnp.sum(sq[2] + jnp.where(self.low, 0.0, sq[1]), axis=-1, keepdims=True)
            f0 = lax.rsqrt(s0 * (1.0 / 192) + 1e-6)
            f1 = lax.rsqrt(s1 * (1.0 / 192) + 1e-6)
            for k, f in enumerate((f0, jnp.where(self.low, f0, f1), f1)):
                n = 3 * px + k
                v = silu_of_half(tiles[k] * f * self.gl_ref[:, 128 * n : 128 * (n + 1)])
                self.keep(n, lo, hi, v)

        cuts = [self.count * c // NCH for c in range(NCH + 1)]
        return [functools.partial(part, lo, hi, px) for px in range(2) for lo, hi in zip(cuts, cuts[1:])]

    def window(self, k, first):
        out = []
        for h in range(2):
            lo = self.sec_ref[k, :, pl.ds(16 + 4 * first + 2 * h, 8, stride=4), :]
            hi = self.sec_ref[k, :, pl.ds(4 * first + 2 * h + 1, 8, stride=4), :]
            out.append(jnp.where(self.half, lo, hi))
        return jnp.concatenate(out, axis=1).astype(BF16)

    def final_steps(self):
        def windows():
            self.s_m = [self.window(k, 0) for k in range(6)]
            self.s_p = [self.window(k, 1) for k in range(6)]
            for px in range(2):
                mixed = jnp.where(self.low, self.s_p[3 * px + 1], self.s_m[3 * px + 1])
                self.s_e += [self.s_p[3 * px], mixed, self.s_m[3 * px + 2]]

        def mul(a, source, kind, lo, even):
            tiles = getattr(self, source)
            if even:
                tiles = [v[1:] for v in tiles[:3]] + [v[:-1] for v in tiles[3:]]
            lhs = jnp.concatenate(tiles, axis=-1).reshape(-1, 768)
            w = self.wf_ref[kind, :, lo : lo + 256]
            self.results[a, even] = jnp.dot(lhs, w, preferred_element_type=F32).reshape(-1, 16, 256)

        plan = ((1, "s_e", 1, 0), (2, "s_e", 1, 256), (0, "s_m", 3, 256), (3, "s_p", 3, 0))
        steps = [windows]
        for a, source, kind, lo in plan:
            steps += [
                functools.partial(mul, a, source, kind, lo, False),
                functools.partial(mul, a, source, kind - 1, lo, True),
                functools.partial(self.place, a),
            ]
        return steps

    def place(self, a):
        o, e = self.results[a, False], self.results[a, True]
        t0 = jnp.where(self.lane < 96, o[:-1, :, 128:], e[..., :128])
        t1 = e[..., 128:]
        t2 = jnp.where(self.lane < 32, e[..., :128], o[1:, :, :128])
        for k, t in enumerate((t0, t1, t2)):
            t = t + self.bf_ref[:, 128 * k : 128 * (k + 1)]
            for u in range(SUB):
                self.rows_ref[3 * (self.sub + u) + k, pl.ds(a, 16, stride=4), :] = t[u]

    def store_steps(self):
        def part(j, t):
            base = 16 * (2 * j + t)
            for n in range(3 * self.sub, 3 * (self.sub + SUB)):
                rows = self.rows_ref[n, base : base + 16, :]
                self.out_ref[2 * t + j, :, 128 * n : 128 * (n + 1)] = rows.astype(BF16)

        return [functools.partial(part, j, t) for j in range(2) for t in range(2)]


def back(step, *refs):
    parts = [Columns(step, sub, *refs) for sub in range(0, XB, SUB)]
    last = len(parts) - 1
    for turn in range(len(parts) + 3):
        lists = []
        if turn <= last:
            lists.append(parts[turn].lift_steps())
        if 0 <= turn - 1 <= last:
            lists.append(parts[turn - 1].norm_steps())
        if 0 <= turn - 2 <= last:
            lists.append(parts[turn - 2].final_steps())
        if 0 <= turn - 3 <= last:
            lists.append(parts[turn - 3].store_steps())
        weave(*lists)


def spread(half):
    wide, narrow = half[:, :128], half[:, 128:]
    return jnp.concatenate([wide, narrow, narrow, wide] * 2, axis=-1)


def decode_kernel(
    above_ref, own_ref, below_ref, band_hbm, bin_ref, gin_ref, wtime_hbm, btime_ref, lift_hbm, blift_ref, glift_ref, final_hbm, bfinal_ref,
    out_ref, grid_ref, dbl_ref, rows_ref, sec_ref, band_ref, wtime_ref, wl_ref, wf_ref, bl_ref, gl_ref, bf_ref, load_sem,
):
    step = pl.program_id(0)

    @pl.when(step == 0)
    def _():
        loads = [
            pltpu.make_async_copy(src, dst, load_sem.at[n])
            for n, (src, dst) in enumerate(
                ((band_hbm, band_ref), (wtime_hbm, wtime_ref), (lift_hbm, wl_ref), (final_hbm, wf_ref))
            )
        ]
        for copy in loads:
            copy.start()
        bl_ref[...] = spread(blift_ref[...].reshape(1, -1))
        gl_ref[...] = 0.5 * spread(glift_ref[...].reshape(1, -1))
        bf_ref[...] = jnp.concatenate([bfinal_ref[...].reshape(1, -1)] * 4, axis=-1)
        front((above_ref, own_ref, below_ref), band_ref, bin_ref, gin_ref, wtime_ref, btime_ref, grid_ref, dbl_ref, loads)
        loads[2].wait()
        loads[3].wait()

    back(step, dbl_ref, wl_ref, bl_ref, gl_ref, wf_ref, bf_ref, out_ref, rows_ref, sec_ref)


def decode(above, own, below, band, wl, wf, b_in, gain_in, w_time, b_time, b_lift, gain_lift, b_final):
    width = 128
    vmem, hbm = pl.BlockSpec(memory_space=pltpu.VMEM), pl.BlockSpec(memory_space=pltpu.HBM)
    w_time = w_time.reshape(-1, w_time.shape[-1])
    weights = (band, w_time, wl, wf)
    return pl.pallas_call(
        decode_kernel,
        grid=(width // XB,),
        in_specs=[vmem, vmem, vmem, hbm, vmem, vmem, hbm, vmem, hbm, vmem, vmem, hbm, vmem],
        out_specs=pl.BlockSpec((4, 16, XB * 384), lambda i: (0, 0, i)),
        out_shape=jax.ShapeDtypeStruct((4, 16, width * 384), BF16),
        scratch_shapes=[
            pltpu.VMEM((6, 18, 8, 128), F32),
            pltpu.VMEM((3, width + 2, 32, 128), F32),
            pltpu.VMEM((XB * 3, 64, 128), F32),
            pltpu.VMEM((XB // SUB, 6, SUB + 1, 56, 128), F32),
        ]
        + [pltpu.VMEM(w.shape, BF16) for w in weights]
        + [pltpu.VMEM((1, 768), F32), pltpu.VMEM((1, 768), F32), pltpu.VMEM((1, 384), F32)]
        + [pltpu.SemaphoreType.DMA((4,))],
        compiler_params=pltpu.CompilerParams(vmem_limit_bytes=VMEM_LIMIT),
        name="decode",
    )(above, own, below, band, b_in, gain_in, w_time, b_time, wl, b_lift, gain_lift, wf, b_final)


def far_first(count):
    return sorted(range(1, count), key=lambda k: -min(k, count - k))


def exchange_kernel(
    rows, frames,
    lat_hbm, slot_hbm, win_hbm, wlift_hbm, wfinal_hbm,
    above, own, below, band_hbm, lift_hbm, final_hbm,
    lat_ref, slot_ref, send1, recv1, send2, recv2, block, win_ref, wlift_ref, wfinal_ref, band_ref, lift_ref, final_ref,
    load_sem, store_sem, send_sem1, recv_sem1, send_sem2, recv_sem2, send_sem3, recv_sem3,
):
    r, f = lax.axis_index("rows"), lax.axis_index("frames")
    loads = [
        pltpu.make_async_copy(src, dst, load_sem.at[n])
        for n, (src, dst) in enumerate(
            (
                (win_hbm, win_ref), (wlift_hbm, wlift_ref), (wfinal_hbm, wfinal_ref),
                (lat_hbm, lat_ref), (slot_hbm, slot_ref),
            )
        )
    ]
    loads[4].start()
    loads[3].start()

    def at(dr, df):
        return {"rows": lax.rem(r + dr + rows, rows), "frames": lax.rem(f + df + frames, frames)}

    near = [(dr, df) for df in range(3) for dr in (0, 1, -1) if (dr, df) != (0, 0)]
    far = [(dr, df) for dr, df in near if dr != 0 and df != 0]
    barrier = pltpu.get_barrier_semaphore()
    sources = [(k, 0) for k in range(1, rows)] + [(0, k) for k in range(1, frames)] + [(-dr, -df) for dr, df in far]
    for dr, df in sources:
        pl.semaphore_signal(barrier, inc=1, device_id=at(dr, df), device_id_type=pl.DeviceIdType.MESH)

    for copy in loads[:3]:
        copy.start()
    loads[4].wait()
    loads[3].wait()

    slots, width = lat_ref.shape
    across = jnp.broadcast_to(slot_ref[...].reshape(1, slots), (slots, slots))
    down = across.T
    index = lax.broadcasted_iota(jnp.int32, (slots, slots), 0)
    lane = lax.broadcasted_iota(jnp.int32, (slots, slots), 1)
    twin = jnp.logical_and(across // slots == down // slots, index < lane)
    rank = jnp.sum(jnp.where(twin, 1, 0), axis=0, keepdims=True)
    target = 2 * (across[:1] // slots) + rank
    total = 2 * rows * frames
    place = lax.broadcasted_iota(jnp.int32, (total, slots), 0) == target
    tags = (down % slots + 1).astype(F32).astype(BF16)
    tagged = jnp.concatenate([lat_ref[...], tags], axis=-1)
    packed = jnp.dot(jnp.where(place, 1.0, 0.0).astype(BF16), tagged, preferred_element_type=F32)
    send1[...] = packed.astype(BF16).reshape(send1.shape)
    recv1[r] = send1[r]
    pl.semaphore_wait(barrier, len(sources))

    def remote(src, dst, send, recv, dr, df):
        return pltpu.make_async_remote_copy(
            src_ref=src, dst_ref=dst, send_sem=send, recv_sem=recv,
            device_id=at(dr, df), device_id_type=pl.DeviceIdType.MESH,
        )

    first = []
    for k in far_first(rows):
        peer, source = lax.rem(r + k, rows), lax.rem(r - k + rows, rows)
        out = remote(send1.at[peer], recv1.at[r], send_sem1.at[k], recv_sem1.at[k], k, 0)
        out.start()
        first.append((out, remote(send1.at[peer], recv1.at[source], send_sem1.at[k], recv_sem1.at[k], k, 0)))
    loads[0].wait()
    make_band(win_ref, band_ref)
    loads[1].wait()
    make_lift(wlift_ref, lift_ref, 0, 0)
    for out, arrival in first:
        arrival.wait_recv()

    o = lax.broadcasted_iota(jnp.int32, (total, total), 0)
    i = lax.broadcasted_iota(jnp.int32, (total, total), 1)
    group = 2 * rows
    regroup = i == ((o // 2) % rows) * (2 * frames) + (o // group) * 2 + o % 2
    moved = jnp.dot(
        jnp.where(regroup, 1.0, 0.0).astype(BF16), recv1[...].reshape(total, 2 * width), preferred_element_type=F32
    )
    send2[...] = moved.astype(BF16).reshape(send2.shape)
    recv2[f] = send2[f]
    second = []
    for k in far_first(frames):
        peer, source = lax.rem(f + k, frames), lax.rem(f - k + frames, frames)
        out = remote(send2.at[peer], recv2.at[f], send_sem2.at[k], recv_sem2.at[k], 0, k)
        out.start()
        second.append((out, remote(send2.at[peer], recv2.at[source], send_sem2.at[k], recv_sem2.at[k], 0, k)))
    make_lift(wlift_ref, lift_ref, 0, 1)
    make_lift(wlift_ref, lift_ref, 1, 0)
    for out, arrival in second:
        arrival.wait_recv()

    arrived = recv2[...].reshape(total, 2 * width)
    want = lax.broadcasted_iota(jnp.int32, (total, slots), 1).astype(F32) + 1.0
    land = jnp.where(arrived[:, width:].astype(F32) == want, 1.0, 0.0).astype(BF16)
    canvas = lax.dot_general(land, arrived[:, :width], (((0,), (0,)), ((), ())), preferred_element_type=F32)
    block[...] = canvas.astype(BF16).reshape(2, 64, width)
    third = []
    for n, (dr, df) in enumerate(near):
        src, region = {
            0: (block, own),
            1: (block.at[:, pl.ds(32, 32)], above),
            -1: (block.at[:, pl.ds(0, 32)], below),
        }[dr]
        out = remote(src, region.at[2 - df], send_sem3.at[n], recv_sem3.at[n], dr, df)
        out.start()
        third.append(out)
    keep = pltpu.make_async_copy(block, own.at[2], load_sem.at[5])
    keep.start()
    make_lift(wlift_ref, lift_ref, 1, 1)
    loads[2].wait()
    for part in range(3):
        make_final(wfinal_ref, final_ref, part)
    stores = [
        pltpu.make_async_copy(src, dst, store_sem.at[n])
        for n, (src, dst) in enumerate(((band_ref, band_hbm), (lift_ref, lift_hbm), (final_ref, final_hbm)))
    ]
    for copy in stores:
        copy.start()
    for out in third:
        out.wait_recv()
    keep.wait()
    for out, _ in first + second:
        out.wait_send()
    for out in third:
        out.wait_send()
    for copy in stores:
        copy.wait()


def exchange(latents, tile_slot, w_in, w_lift, w_final):
    rows, frames = lax.axis_size("rows"), lax.axis_size("frames")
    width = latents.shape[1]
    hbm = pl.BlockSpec(memory_space=pltpu.HBM)
    weights = (w_in, w_lift.swapaxes(2, 3), w_final)
    made = [(768, 768), (1536, 768), (4, 768, 512)]
    blocks = [(3, 2, 32, width), (3, 2, 64, width), (3, 2, 32, width)]
    dma = pltpu.SemaphoreType.DMA
    return pl.pallas_call(
        functools.partial(exchange_kernel, rows, frames),
        in_specs=[hbm] * 5,
        out_specs=[hbm] * 6,
        out_shape=[jax.ShapeDtypeStruct(shape, BF16) for shape in blocks + made],
        scratch_shapes=[
            pltpu.VMEM(latents.shape, BF16),
            pltpu.VMEM(tile_slot.shape, jnp.int32),
            pltpu.VMEM((rows, 2 * frames, 2 * width), BF16),
            pltpu.VMEM((rows, 2 * frames, 2 * width), BF16),
            pltpu.VMEM((frames, 2 * rows, 2 * width), BF16),
            pltpu.VMEM((frames, 2 * rows, 2 * width), BF16),
            pltpu.VMEM((2, 64, width), BF16),
        ]
        + [pltpu.VMEM(w.shape, BF16) for w in weights]
        + [pltpu.VMEM(shape, BF16) for shape in made]
        + [dma((6,)), dma((3,)), dma((rows,)), dma((rows,)), dma((frames,)), dma((frames,)), dma((8,)), dma((8,))],
        compiler_params=pltpu.CompilerParams(
            collective_id=0, has_side_effects=True, vmem_limit_bytes=VMEM_LIMIT
        ),
        name="exchange",
    )(latents, tile_slot, *weights)


def shards(
    latents, tile_slot, w_in, b_in, gain_in, w_time, b_time, w_lift, b_lift, gain_lift, w_final, b_final
):
    above, own, below, band, wl, wf = exchange(latents, tile_slot, w_in, w_lift, w_final)
    return decode(above, own, below, band, wl, wf, b_in, gain_in, w_time, b_time, b_lift, gain_lift, b_final)


def solution(mesh):
    in_specs = (P(("rows", "frames"), None), P(("rows", "frames"))) + (P(),) * 10
    out_specs = P("frames", "rows", None)
    return jax.shard_map(shards, mesh=mesh, in_specs=in_specs, out_specs=out_specs, check_vma=False)
```

```python
import functools

import jax
import jax.numpy as jnp
from jax import lax
from jax.experimental import pallas as pl
from jax.experimental.pallas import tpu as pltpu
from jax.sharding import PartitionSpec as P

BF16, F32 = jnp.bfloat16, jnp.float32
XB = 64
NCH = 3
SUB = 32
SC = 8
VMEM_LIMIT = 60 * 1024 * 1024


def silu_of_half(half):
    return half + half * jnp.tanh(half)


def pick(parts, tap, phase):
    if phase == 0:
        return parts[0] + parts[1] if tap == 0 else parts[2]
    return parts[0] if tap == 0 else parts[1] + parts[2]


def summed_taps(load, ty, tx, py, px):
    rows = [pick([load(dy, dx) for dy in range(3)], ty, py) for dx in range(3)]
    return pick(rows, tx, px)


def make_band(win_ref, band_ref):
    channels = win_ref.shape[-1]
    band_ref[...] = jnp.zeros_like(band_ref)
    for k in range(3):
        for dy in range(3):
            for dx in range(3):
                taps = win_ref[k, dy, dx]
                for pp in range(2):
                    row = 256 * k + 64 * dy + 16 * (dx + pp)
                    band_ref[row : row + 16, channels * pp : channels * (pp + 1)] = taps


def make_lift(wlift_ref, lift_ref, ty, tx):
    depth = wlift_ref.shape[-1]

    def part(lo, hi, py, px):
        return summed_taps(lambda dy, dx: wlift_ref[dy, dx, lo:hi, :].astype(F32), ty, tx, py, px)

    for px in range(2):
        tiles = [
            part(0, 128, 0, px),
            jnp.concatenate([part(128, 192, 0, px), part(128, 192, 1, px)], axis=0),
            part(0, 128, 1, px),
        ]
        for n, tile in enumerate(tiles):
            lane = 384 * px + 128 * n
            row = depth * (2 * ty + tx)
            lift_ref[row : row + depth, lane : lane + 128] = tile.T.astype(BF16)


def make_final(wfinal_ref, final_ref, part):
    rows = slice(64 * part, 64 * (part + 1))
    low = lax.broadcasted_iota(jnp.int32, (64, 128), 1) < 64
    pad = jnp.zeros((64, 32), F32)

    def load(dy, dx):
        return wfinal_ref[dy, dx, rows, :].astype(F32)

    for ty in range(2):
        for tx in range(2):
            for qy in range(2):
                q0, q1 = (jnp.concatenate([summed_taps(load, ty, tx, qy, qx), pad], axis=-1) for qx in range(2))
                r0, r1 = pltpu.roll(q0, 96, 1), pltpu.roll(q1, 64, 1)
                pairs = ((jnp.where(low, r1, r0), jnp.where(low, r0, r1)), (pltpu.roll(q0, 32, 1), q1))
                for xpar, tiles in enumerate(pairs):
                    px = tx if xpar else 1 - tx
                    for jpar in range(2):
                        py = ty if jpar else 1 - ty
                        slot = 384 * px + (256 * py + 64 * part if part < 2 else 128 + 64 * py)
                        for n, tile in enumerate(tiles):
                            lane = 256 * qy + 128 * n
                            final_ref[2 * jpar + xpar, slot : slot + 64, lane : lane + 128] = tile.astype(BF16)


def weave(*lists):
    order = sorted(
        ((n + 0.5) / len(steps), which, n) for which, steps in enumerate(lists) for n in range(len(steps))
    )
    for _, which, n in order:
        lists[which][n]()


def front(block_refs, band_ref, bin_ref, gin_ref, wtime_ref, btime_ref, grid_ref, dbl_ref, waits):
    row, frame = lax.axis_index("rows"), lax.axis_index("frames")
    top, bottom = row == 0, row == lax.axis_size("rows") - 1
    out_row = lax.broadcasted_iota(jnp.int32, (256, 256), 0)
    in_row = lax.broadcasted_iota(jnp.int32, (256, 256), 1)
    t, s, y = out_row // 128, (out_row // 8) % 16, out_row % 8
    wanted = jnp.where(
        y < 2,
        32 * t + 16 * y + s,
        jnp.where(y < 6, 64 + 64 * t + 16 * (y - 2) + s, 192 + 32 * t + 16 * (y - 6) + s),
    )
    inside = jnp.logical_and(
        jnp.logical_or(jnp.logical_not(top), y >= 2), jnp.logical_or(jnp.logical_not(bottom), y < 6)
    )
    chosen = jnp.logical_and(in_row == wanted, inside)
    zero_col = jnp.zeros((6, 1, 8, 128), F32)
    grid_ref[:, 0:1] = zero_col
    grid_ref[:, 17:18] = zero_col
    for part in range(3):
        select = jnp.where(jnp.logical_and(chosen, frame + part >= 2), 1.0, 0.0).astype(BF16)
        cells = jnp.concatenate([ref[part].reshape(-1, 128) for ref in block_refs], axis=0)
        picked = jnp.dot(select, cells, preferred_element_type=F32)
        grid_ref[2 * part : 2 * part + 2, 1:17] = picked.reshape(2, 16, 8, 128)

    lane = lax.broadcasted_iota(jnp.int32, (1, 1, 1, 128), 3)
    sub = lax.broadcasted_iota(jnp.int32, (1, 1, 8, 1), 2)
    edge_col = jnp.zeros((3, 1, 32, 128), F32)
    dbl_ref[:, 0:1] = edge_col
    dbl_ref[:, dbl_ref.shape[1] - 1 :] = edge_col

    b_in, g_in, b_time = (v[...].reshape(1, -1) for v in (bin_ref, gin_ref, btime_ref))
    g_in = 0.5 * g_in

    def chunk(s0):
        pieces, hidden, feats, hist = [], [], [], []

        def build(q):
            flat = grid_ref[:, s0 : s0 + SC + 2].reshape(6 * (SC + 2), 8, 128)
            turned = [flat, pltpu.roll(flat, 7, 1), pltpu.roll(flat, 6, 1)]
            shift = (16 - 32 * q) % 128
            parts = []
            for d, lanes in enumerate((shift, shift + 64, shift)):
                moved = pltpu.roll(turned[d], lanes % 128, 2).reshape(6, SC + 2, 8, 128)
                own = moved[:, 1:-1]
                at = 64 * (d % 2)
                if q == 0:
                    own = jnp.where((lane >= at) & (lane < at + 16), moved[:, :-2], own)
                if q == 3:
                    own = jnp.where((lane >= at + 48) & (lane < at + 64), moved[:, 2:], own)
                parts.append(own)
            first = jnp.where(lane < 64, parts[0], parts[1])
            pieces.append(jnp.concatenate([first, parts[2]], axis=-1))

        def gather():
            patch = jnp.stack(pieces, axis=2).reshape(6, SC * 4 * 8, 256).astype(BF16)
            patch = jnp.concatenate([patch[k : k + 4] for k in range(3)], axis=-1)
            pieces.append(patch.reshape(4 * SC * 32, 768))

        def expand(n):
            out = jnp.dot(pieces[-1], band_ref[:, 256 * n : 256 * (n + 1)], preferred_element_type=F32)
            hidden.append(out.reshape(4, SC * 32, 256))

        def norm(t):
            tiles = []
            for pp in range(2):
                h = []
                for k in range(3):
                    n = 3 * pp + k
                    lanes = slice(128 * (n % 2), 128 * (n % 2) + 128)
                    h.append(hidden[n // 2][t][:, lanes] + b_in[:, 128 * k : 128 * (k + 1)])
                mean = jnp.sum(h[0] * h[0] + h[1] * h[1] + h[2] * h[2], axis=-1, keepdims=True) * (1.0 / 384)
                factor = lax.rsqrt(mean + 1e-6)
                tiles.append([silu_of_half(h[k] * factor * g_in[:, 128 * k : 128 * (k + 1)]) for k in range(3)])
            merged = []
            for k in range(3):
                v = jnp.stack([tiles[pp][k].reshape(SC * 4, 8, 128) for pp in range(2)], axis=1)
                if t < 2:
                    v = jnp.where(frame > 0, v, 0.0)
                merged.append(v.reshape(SC * 64, 128).astype(BF16))
            feats.append(merged)

        def align():
            rows = [jnp.concatenate([v for k in range(3) for v in feats[t + k]], axis=-1) for t in range(2)]
            hist.append(jnp.concatenate(rows, axis=0))

        def double(n):
            acc = jnp.dot(hist[0], wtime_ref[:, 256 * n : 256 * (n + 1)], preferred_element_type=F32)
            acc = (acc + b_time[:, 256 * n : 256 * (n + 1)]).reshape(2, SC * 8, 8, 256)
            for i in range(2):
                j, k = (2 * n + i) // 3, (2 * n + i) % 3
                for t in range(2):
                    lanes = acc[t, :, :, 128 * i : 128 * (i + 1)]
                    dbl_ref[k, 8 * s0 + 1 : 8 * (s0 + SC) + 1, pl.ds(2 * j + t, 8, stride=4), :] = lanes

        return (
            [functools.partial(build, q) for q in range(4)] + [gather] + [functools.partial(expand, n) for n in range(3)],
            [functools.partial(norm, t) for t in range(4)],
            [align] + [functools.partial(double, n) for n in range(3)],
        )

    chunks = [chunk(s0) for s0 in range(0, 16, SC)]
    for turn in range(len(chunks) + 2):
        if turn in waits:
            waits[turn].wait()
        weave(*(chunks[turn - n][n] for n in range(3) if 0 <= turn - n < len(chunks)))

    @pl.when(top)
    def _():
        dbl_ref[:, :, 0:4, :] = jnp.zeros((3, dbl_ref.shape[1], 4, 128), F32)

    @pl.when(bottom)
    def _():
        dbl_ref[:, :, 20:24, :] = jnp.zeros((3, dbl_ref.shape[1], 4, 128), F32)


class Columns:
    def __init__(self, step, sub, dbl_ref, wl_ref, bl_ref, gl_ref, wf_ref, bf_ref, out_ref, rows_ref, sec_ref):
        row = lax.axis_index("rows")
        self.top, self.bottom = row == 0, row == lax.axis_size("rows") - 1
        self.width = dbl_ref.shape[1] - 2
        self.x0, self.sub, self.count = step * XB + sub, sub, SUB + 1
        self.low = lax.broadcasted_iota(jnp.int32, (1, 1, 128), 2) < 64
        self.lane = lax.broadcasted_iota(jnp.int32, (1, 1, 128), 2)
        self.half = lax.broadcasted_iota(jnp.int32, (1, 8, 1), 1) < 4
        self.dbl_ref, self.wl_ref, self.bl_ref, self.gl_ref = dbl_ref, wl_ref, bl_ref, gl_ref
        self.wf_ref, self.bf_ref, self.out_ref, self.rows_ref = wf_ref, bf_ref, out_ref, rows_ref
        self.sec_ref = sec_ref.at[sub // SUB]
        self.acc, self.results, self.s_m, self.s_p, self.s_e = {}, {}, [], [], []

    def load(self):
        patch = []
        for ty in range(2):
            tiles = [self.dbl_ref[k, pl.ds(self.x0, self.count + 1), 4 * ty : 4 * ty + 24, :] for k in range(3)]
            patch += [
                v[tx : tx + self.count].reshape(self.count * 24, 128).astype(BF16) for tx in range(2) for v in tiles
            ]
        self.patch = jnp.concatenate(patch, axis=-1)

    def lift_steps(self):
        def part(n):
            w = self.wl_ref[:, 256 * n : 256 * (n + 1)]
            acc = jnp.dot(self.patch, w, preferred_element_type=F32)
            self.acc[n] = acc.reshape(self.count, 24, 256)

        return [self.load] + [functools.partial(part, n) for n in range(3)]

    def keep(self, n, lo, hi, v):
        px, k = n // 3, n % 3
        first_rows = lax.broadcasted_iota(jnp.int32, (1, 8, 1), 1) < 4
        above, below = jnp.logical_and(first_rows, self.top), jnp.logical_and(first_rows, self.bottom)
        for g in range(3):
            part = v[:, 8 * g : 8 * (g + 1)]
            if g == 0 and k < 2:
                part = jnp.where(above if k == 0 else jnp.logical_and(above, self.low), 0.0, part)
            if g == 2 and k > 0:
                part = jnp.where(below if k == 2 else jnp.logical_and(below, jnp.logical_not(self.low)), 0.0, part)
            rows = slice(16 + 8 * g, 24 + 8 * g)
            if px == 0 and lo == 0:
                self.sec_ref[n, 0:1, rows, :] = jnp.where(self.x0 == 0, 0.0, part[0:1])
                self.sec_ref[n, 1:hi, rows, :] = part[1:]
            elif px == 1 and hi == self.count:
                self.sec_ref[n, lo : hi - 1, rows, :] = part[:-1]
                self.sec_ref[n, hi - 1 : hi, rows, :] = jnp.where(self.x0 == self.width - SUB, 0.0, part[-1:])
            else:
                self.sec_ref[n, lo:hi, rows, :] = part

    def norm_steps(self):
        def part(lo, hi, px):
            tiles = []
            for k in range(3):
                n = 3 * px + k
                lanes = slice(128 * (n % 2), 128 * (n % 2) + 128)
                tiles.append(self.acc[n // 2][lo:hi, :, lanes] + self.bl_ref[:, 128 * n : 128 * (n + 1)])
            sq = [v * v for v in tiles]
            s0 = jnp.sum(sq[0] + jnp.where(self.low, sq[1], 0.0), axis=-1, keepdims=True)
            s1 = jnp.sum(sq[2] + jnp.where(self.low, 0.0, sq[1]), axis=-1, keepdims=True)
            f0 = lax.rsqrt(s0 * (1.0 / 192) + 1e-6)
            f1 = lax.rsqrt(s1 * (1.0 / 192) + 1e-6)
            for k, f in enumerate((f0, jnp.where(self.low, f0, f1), f1)):
                n = 3 * px + k
                v = silu_of_half(tiles[k] * f * self.gl_ref[:, 128 * n : 128 * (n + 1)])
                self.keep(n, lo, hi, v)

        cuts = [self.count * c // NCH for c in range(NCH + 1)]
        return [functools.partial(part, lo, hi, px) for px in range(2) for lo, hi in zip(cuts, cuts[1:])]

    def window(self, k, first):
        out = []
        for h in range(2):
            lo = self.sec_ref[k, :, pl.ds(16 + 4 * first + 2 * h, 8, stride=4), :]
            hi = self.sec_ref[k, :, pl.ds(4 * first + 2 * h + 1, 8, stride=4), :]
            out.append(jnp.where(self.half, lo, hi))
        return jnp.concatenate(out, axis=1).astype(BF16)

    def final_steps(self):
        def windows():
            self.s_m = [self.window(k, 0) for k in range(6)]
            self.s_p = [self.window(k, 1) for k in range(6)]
            for px in range(2):
                mixed = jnp.where(self.low, self.s_p[3 * px + 1], self.s_m[3 * px + 1])
                self.s_e += [self.s_p[3 * px], mixed, self.s_m[3 * px + 2]]

        def mul(a, source, kind, lo, even):
            tiles = getattr(self, source)
            if even:
                tiles = [v[1:] for v in tiles[:3]] + [v[:-1] for v in tiles[3:]]
            lhs = jnp.concatenate(tiles, axis=-1).reshape(-1, 768)
            w = self.wf_ref[kind, :, lo : lo + 256]
            self.results[a, even] = jnp.dot(lhs, w, preferred_element_type=F32).reshape(-1, 16, 256)

        plan = ((1, "s_e", 1, 0), (2, "s_e", 1, 256), (0, "s_m", 3, 256), (3, "s_p", 3, 0))
        steps = [windows]
        for a, source, kind, lo in plan:
            steps += [
                functools.partial(mul, a, source, kind, lo, False),
                functools.partial(mul, a, source, kind - 1, lo, True),
                functools.partial(self.place, a),
            ]
        return steps

    def place(self, a):
        o, e = self.results[a, False], self.results[a, True]
        t0 = jnp.where(self.lane < 96, o[:-1, :, 128:], e[..., :128])
        t1 = e[..., 128:]
        t2 = jnp.where(self.lane < 32, e[..., :128], o[1:, :, :128])
        for k, t in enumerate((t0, t1, t2)):
            t = t + self.bf_ref[:, 128 * k : 128 * (k + 1)]
            for u in range(SUB):
                self.rows_ref[3 * (self.sub + u) + k, pl.ds(a, 16, stride=4), :] = t[u]

    def store_steps(self):
        def part(j, t):
            base = 16 * (2 * j + t)
            for n in range(3 * self.sub, 3 * (self.sub + SUB)):
                rows = self.rows_ref[n, base : base + 16, :]
                self.out_ref[2 * t + j, :, 128 * n : 128 * (n + 1)] = rows.astype(BF16)

        return [functools.partial(part, j, t) for j in range(2) for t in range(2)]


def back(step, *refs):
    parts = [Columns(step, sub, *refs) for sub in range(0, XB, SUB)]
    last = len(parts) - 1
    for turn in range(len(parts) + 3):
        lists = []
        if turn <= last:
            lists.append(parts[turn].lift_steps())
        if 0 <= turn - 1 <= last:
            lists.append(parts[turn - 1].norm_steps())
        if 0 <= turn - 2 <= last:
            lists.append(parts[turn - 2].final_steps())
        if 0 <= turn - 3 <= last:
            lists.append(parts[turn - 3].store_steps())
        weave(*lists)


def spread(half):
    wide, narrow = half[:, :128], half[:, 128:]
    return jnp.concatenate([wide, narrow, narrow, wide] * 2, axis=-1)


def decode_kernel(count, *refs):
    sources, out_ref, copies = refs[:count], refs[count], refs[count + 1 : 2 * count + 1]
    grid_ref, dbl_ref, rows_ref, sec_ref, bl_ref, gl_ref, bf_ref, load_sem = refs[2 * count + 1 :]
    blocks, (bin_ref, gin_ref, btime_ref, blift_ref, glift_ref, bfinal_ref) = copies[:3], copies[3:9]
    band_ref, wtime_ref, wl_ref, wf_ref = copies[9:]
    step = pl.program_id(0)

    @pl.when(step == 0)
    def _():
        loads = [pltpu.make_async_copy(src, dst, load_sem.at[n]) for n, (src, dst) in enumerate(zip(sources, copies))]
        for copy in loads:
            copy.start()
        for copy in loads[:9]:
            copy.wait()
        bl_ref[...] = spread(blift_ref[...].reshape(1, -1))
        gl_ref[...] = 0.5 * spread(glift_ref[...].reshape(1, -1))
        bf_ref[...] = jnp.concatenate([bfinal_ref[...].reshape(1, -1)] * 4, axis=-1)
        waits = {0: loads[9], 2: loads[10]}
        front(blocks, band_ref, bin_ref, gin_ref, wtime_ref, btime_ref, grid_ref, dbl_ref, waits)
        loads[11].wait()
        loads[12].wait()

    back(step, dbl_ref, wl_ref, bl_ref, gl_ref, wf_ref, bf_ref, out_ref, rows_ref, sec_ref)


def decode(above, own, below, band, wl, wf, b_in, gain_in, w_time, b_time, b_lift, gain_lift, b_final):
    width = 128
    hbm = pl.BlockSpec(memory_space=pltpu.HBM)
    w_time = w_time.reshape(-1, w_time.shape[-1])
    args = (above, own, below, b_in, gain_in, b_time, b_lift, gain_lift, b_final, band, w_time, wl, wf)
    return pl.pallas_call(
        functools.partial(decode_kernel, len(args)),
        grid=(width // XB,),
        in_specs=[hbm] * len(args),
        out_specs=pl.BlockSpec((4, 16, XB * 384), lambda i: (0, 0, i)),
        out_shape=jax.ShapeDtypeStruct((4, 16, width * 384), BF16),
        scratch_shapes=[pltpu.VMEM(v.shape, v.dtype) for v in args]
        + [
            pltpu.VMEM((6, 18, 8, 128), F32),
            pltpu.VMEM((3, width + 2, 32, 128), F32),
            pltpu.VMEM((XB * 3, 64, 128), F32),
            pltpu.VMEM((XB // SUB, 6, SUB + 1, 56, 128), F32),
            pltpu.VMEM((1, 768), F32),
            pltpu.VMEM((1, 768), F32),
            pltpu.VMEM((1, 384), F32),
            pltpu.SemaphoreType.DMA((len(args),)),
        ],
        compiler_params=pltpu.CompilerParams(vmem_limit_bytes=VMEM_LIMIT),
        name="decode",
    )(*args)


def far_first(count):
    return sorted(range(1, count), key=lambda k: -min(k, count - k))


def exchange_kernel(
    rows, frames,
    lat_hbm, slot_hbm, win_hbm, wlift_hbm, wfinal_hbm,
    above, own, below, band_hbm, lift_hbm, final_hbm,
    lat_ref, slot_ref, send1, recv1, send2, recv2, block, win_ref, wlift_ref, wfinal_ref, band_ref, lift_ref, final_ref,
    load_sem, store_sem, send_sem1, recv_sem1, send_sem2, recv_sem2, send_sem3, recv_sem3,
):
    r, f = lax.axis_index("rows"), lax.axis_index("frames")
    loads = [
        pltpu.make_async_copy(src, dst, load_sem.at[n])
        for n, (src, dst) in enumerate(
            (
                (win_hbm, win_ref), (wlift_hbm, wlift_ref), (wfinal_hbm, wfinal_ref),
                (lat_hbm, lat_ref), (slot_hbm, slot_ref),
            )
        )
    ]
    loads[4].start()
    loads[3].start()

    def at(dr, df):
        return {"rows": lax.rem(r + dr + rows, rows), "frames": lax.rem(f + df + frames, frames)}

    near = [(dr, df) for df in range(3) for dr in (0, 1, -1) if (dr, df) != (0, 0)]
    far = [(dr, df) for dr, df in near if dr != 0 and df != 0]
    barrier = pltpu.get_barrier_semaphore()
    sources = [(k, 0) for k in range(1, rows)] + [(0, k) for k in range(1, frames)] + [(-dr, -df) for dr, df in far]
    for dr, df in sources:
        pl.semaphore_signal(barrier, inc=1, device_id=at(dr, df), device_id_type=pl.DeviceIdType.MESH)

    for copy in loads[:3]:
        copy.start()
    loads[4].wait()
    loads[3].wait()

    slots, width = lat_ref.shape
    across = jnp.broadcast_to(slot_ref[...].reshape(1, slots), (slots, slots))
    down = across.T
    index = lax.broadcasted_iota(jnp.int32, (slots, slots), 0)
    lane = lax.broadcasted_iota(jnp.int32, (slots, slots), 1)
    twin = jnp.logical_and(across // slots == down // slots, index < lane)
    rank = jnp.sum(jnp.where(twin, 1, 0), axis=0, keepdims=True)
    target = 2 * (across[:1] // slots) + rank
    total = 2 * rows * frames
    place = lax.broadcasted_iota(jnp.int32, (total, slots), 0) == target
    tags = (down % slots + 1).astype(F32).astype(BF16)
    tagged = jnp.concatenate([lat_ref[...], tags], axis=-1)
    packed = jnp.dot(jnp.where(place, 1.0, 0.0).astype(BF16), tagged, preferred_element_type=F32)
    send1[...] = packed.astype(BF16).reshape(send1.shape)
    recv1[r] = send1[r]
    pl.semaphore_wait(barrier, len(sources))

    def remote(src, dst, send, recv, dr, df):
        return pltpu.make_async_remote_copy(
            src_ref=src, dst_ref=dst, send_sem=send, recv_sem=recv,
            device_id=at(dr, df), device_id_type=pl.DeviceIdType.MESH,
        )

    first = []
    for k in far_first(rows):
        peer, source = lax.rem(r + k, rows), lax.rem(r - k + rows, rows)
        out = remote(send1.at[peer], recv1.at[r], send_sem1.at[k], recv_sem1.at[k], k, 0)
        out.start()
        first.append((out, remote(send1.at[peer], recv1.at[source], send_sem1.at[k], recv_sem1.at[k], k, 0)))
    loads[0].wait()
    make_band(win_ref, band_ref)
    loads[1].wait()
    make_lift(wlift_ref, lift_ref, 0, 0)
    for out, arrival in first:
        arrival.wait_recv()

    o = lax.broadcasted_iota(jnp.int32, (total, total), 0)
    i = lax.broadcasted_iota(jnp.int32, (total, total), 1)
    group = 2 * rows
    regroup = i == ((o // 2) % rows) * (2 * frames) + (o // group) * 2 + o % 2
    moved = jnp.dot(
        jnp.where(regroup, 1.0, 0.0).astype(BF16), recv1[...].reshape(total, 2 * width), preferred_element_type=F32
    )
    send2[...] = moved.astype(BF16).reshape(send2.shape)
    recv2[f] = send2[f]
    second = []
    for k in far_first(frames):
        peer, source = lax.rem(f + k, frames), lax.rem(f - k + frames, frames)
        out = remote(send2.at[peer], recv2.at[f], send_sem2.at[k], recv_sem2.at[k], 0, k)
        out.start()
        second.append((out, remote(send2.at[peer], recv2.at[source], send_sem2.at[k], recv_sem2.at[k], 0, k)))
    make_lift(wlift_ref, lift_ref, 0, 1)
    make_lift(wlift_ref, lift_ref, 1, 0)
    for out, arrival in second:
        arrival.wait_recv()

    arrived = recv2[...].reshape(total, 2 * width)
    want = lax.broadcasted_iota(jnp.int32, (total, slots), 1).astype(F32) + 1.0
    land = jnp.where(arrived[:, width:].astype(F32) == want, 1.0, 0.0).astype(BF16)
    canvas = lax.dot_general(land, arrived[:, :width], (((0,), (0,)), ((), ())), preferred_element_type=F32)
    block[...] = canvas.astype(BF16).reshape(2, 64, width)
    third = []
    for n, (dr, df) in enumerate(near):
        src, region = {
            0: (block, own),
            1: (block.at[:, pl.ds(32, 32)], above),
            -1: (block.at[:, pl.ds(0, 32)], below),
        }[dr]
        out = remote(src, region.at[2 - df], send_sem3.at[n], recv_sem3.at[n], dr, df)
        out.start()
        third.append(out)
    keep = pltpu.make_async_copy(block, own.at[2], load_sem.at[5])
    keep.start()
    make_lift(wlift_ref, lift_ref, 1, 1)
    loads[2].wait()
    for part in range(3):
        make_final(wfinal_ref, final_ref, part)
    stores = [
        pltpu.make_async_copy(src, dst, store_sem.at[n])
        for n, (src, dst) in enumerate(((band_ref, band_hbm), (lift_ref, lift_hbm), (final_ref, final_hbm)))
    ]
    for copy in stores:
        copy.start()
    for out in third:
        out.wait_recv()
    keep.wait()
    for out, _ in first + second:
        out.wait_send()
    for out in third:
        out.wait_send()
    for copy in stores:
        copy.wait()


def exchange(latents, tile_slot, w_in, w_lift, w_final):
    rows, frames = lax.axis_size("rows"), lax.axis_size("frames")
    width = latents.shape[1]
    hbm = pl.BlockSpec(memory_space=pltpu.HBM)
    weights = (w_in, w_lift.swapaxes(2, 3), w_final)
    made = [(768, 768), (1536, 768), (4, 768, 512)]
    blocks = [(3, 2, 32, width), (3, 2, 64, width), (3, 2, 32, width)]
    dma = pltpu.SemaphoreType.DMA
    return pl.pallas_call(
        functools.partial(exchange_kernel, rows, frames),
        in_specs=[hbm] * 5,
        out_specs=[hbm] * 6,
        out_shape=[jax.ShapeDtypeStruct(shape, BF16) for shape in blocks + made],
        scratch_shapes=[
            pltpu.VMEM(latents.shape, BF16),
            pltpu.VMEM(tile_slot.shape, jnp.int32),
            pltpu.VMEM((rows, 2 * frames, 2 * width), BF16),
            pltpu.VMEM((rows, 2 * frames, 2 * width), BF16),
            pltpu.VMEM((frames, 2 * rows, 2 * width), BF16),
            pltpu.VMEM((frames, 2 * rows, 2 * width), BF16),
            pltpu.VMEM((2, 64, width), BF16),
        ]
        + [pltpu.VMEM(w.shape, BF16) for w in weights]
        + [pltpu.VMEM(shape, BF16) for shape in made]
        + [dma((6,)), dma((3,)), dma((rows,)), dma((rows,)), dma((frames,)), dma((frames,)), dma((8,)), dma((8,))],
        compiler_params=pltpu.CompilerParams(
            collective_id=0, has_side_effects=True, vmem_limit_bytes=VMEM_LIMIT
        ),
        name="exchange",
    )(latents, tile_slot, *weights)


def shards(
    latents, tile_slot, w_in, b_in, gain_in, w_time, b_time, w_lift, b_lift, gain_lift, w_final, b_final
):
    above, own, below, band, wl, wf = exchange(latents, tile_slot, w_in, w_lift, w_final)
    return decode(above, own, below, band, wl, wf, b_in, gain_in, w_time, b_time, b_lift, gain_lift, b_final)


def solution(mesh):
    in_specs = (P(("rows", "frames"), None), P(("rows", "frames"))) + (P(),) * 10
    out_specs = P("frames", "rows", None)
    return jax.shard_map(shards, mesh=mesh, in_specs=in_specs, out_specs=out_specs, check_vma=False)
```

```python
import functools

import jax
import jax.numpy as jnp
from jax import lax
from jax.experimental import pallas as pl
from jax.experimental.pallas import tpu as pltpu
from jax.sharding import PartitionSpec as P

BF16, F32 = jnp.bfloat16, jnp.float32
XB = 64
NCH = 3
SUB = 32
SC = 8
VMEM_LIMIT = 60 * 1024 * 1024


def silu_of_half(half):
    return half + half * jnp.tanh(half)


def pick(parts, tap, phase):
    if phase == 0:
        return parts[0] + parts[1] if tap == 0 else parts[2]
    return parts[0] if tap == 0 else parts[1] + parts[2]


def summed_taps(load, ty, tx, py, px):
    rows = [pick([load(dy, dx) for dy in range(3)], ty, py) for dx in range(3)]
    return pick(rows, tx, px)


def make_band(win_ref, band_ref):
    channels = win_ref.shape[-1]
    band_ref[...] = jnp.zeros_like(band_ref)
    for k in range(3):
        for dy in range(3):
            for dx in range(3):
                taps = win_ref[k, dy, dx]
                for pp in range(2):
                    row = 256 * k + 64 * dy + 16 * (dx + pp)
                    band_ref[row : row + 16, channels * pp : channels * (pp + 1)] = taps


def make_lift(wlift_ref, lift_ref, ty, tx):
    depth = wlift_ref.shape[-1]

    def part(lo, hi, py, px):
        return summed_taps(lambda dy, dx: wlift_ref[dy, dx, lo:hi, :].astype(F32), ty, tx, py, px)

    for px in range(2):
        tiles = [
            part(0, 128, 0, px),
            jnp.concatenate([part(128, 192, 0, px), part(128, 192, 1, px)], axis=0),
            part(0, 128, 1, px),
        ]
        for n, tile in enumerate(tiles):
            lane = 384 * px + 128 * n
            row = depth * (2 * ty + tx)
            lift_ref[row : row + depth, lane : lane + 128] = tile.T.astype(BF16)


def make_final(wfinal_ref, final_ref, part):
    rows = slice(64 * part, 64 * (part + 1))
    low = lax.broadcasted_iota(jnp.int32, (64, 128), 1) < 64
    pad = jnp.zeros((64, 32), F32)

    def load(dy, dx):
        return wfinal_ref[dy, dx, rows, :].astype(F32)

    for ty in range(2):
        for tx in range(2):
            for qy in range(2):
                q0, q1 = (jnp.concatenate([summed_taps(load, ty, tx, qy, qx), pad], axis=-1) for qx in range(2))
                r0, r1 = pltpu.roll(q0, 96, 1), pltpu.roll(q1, 64, 1)
                pairs = ((jnp.where(low, r1, r0), jnp.where(low, r0, r1)), (pltpu.roll(q0, 32, 1), q1))
                for xpar, tiles in enumerate(pairs):
                    px = tx if xpar else 1 - tx
                    for jpar in range(2):
                        py = ty if jpar else 1 - ty
                        slot = 384 * px + (256 * py + 64 * part if part < 2 else 128 + 64 * py)
                        for n, tile in enumerate(tiles):
                            lane = 256 * qy + 128 * n
                            final_ref[2 * jpar + xpar, slot : slot + 64, lane : lane + 128] = tile.astype(BF16)


def weave(*lists):
    order = sorted(
        ((n + 0.5) / len(steps), which, n) for which, steps in enumerate(lists) for n in range(len(steps))
    )
    for _, which, n in order:
        lists[which][n]()


def front(block_refs, band_ref, bin_ref, gin_ref, wtime_ref, btime_ref, grid_ref, dbl_ref, waits):
    row, frame = lax.axis_index("rows"), lax.axis_index("frames")
    top, bottom = row == 0, row == lax.axis_size("rows") - 1
    out_row = lax.broadcasted_iota(jnp.int32, (256, 256), 0)
    in_row = lax.broadcasted_iota(jnp.int32, (256, 256), 1)
    t, s, y = out_row // 128, (out_row // 8) % 16, out_row % 8
    wanted = jnp.where(
        y < 2,
        32 * t + 16 * y + s,
        jnp.where(y < 6, 64 + 64 * t + 16 * (y - 2) + s, 192 + 32 * t + 16 * (y - 6) + s),
    )
    inside = jnp.logical_and(
        jnp.logical_or(jnp.logical_not(top), y >= 2), jnp.logical_or(jnp.logical_not(bottom), y < 6)
    )
    chosen = jnp.logical_and(in_row == wanted, inside)
    zero_col = jnp.zeros((6, 1, 8, 128), F32)
    grid_ref[:, 0:1] = zero_col
    grid_ref[:, 17:18] = zero_col
    for part in range(3):
        select = jnp.where(jnp.logical_and(chosen, frame + part >= 2), 1.0, 0.0).astype(BF16)
        cells = jnp.concatenate([ref[part].reshape(-1, 128) for ref in block_refs], axis=0)
        picked = jnp.dot(select, cells, preferred_element_type=F32)
        grid_ref[2 * part : 2 * part + 2, 1:17] = picked.reshape(2, 16, 8, 128)

    lane = lax.broadcasted_iota(jnp.int32, (1, 1, 1, 128), 3)
    sub = lax.broadcasted_iota(jnp.int32, (1, 1, 8, 1), 2)
    edge_col = jnp.zeros((3, 1, 32, 128), F32)
    dbl_ref[:, 0:1] = edge_col
    dbl_ref[:, dbl_ref.shape[1] - 1 :] = edge_col

    b_in, g_in, b_time = (v[...].reshape(1, -1) for v in (bin_ref, gin_ref, btime_ref))
    g_in = 0.5 * g_in

    def chunk(s0):
        pieces, hidden, feats, hist = [], [], [], []

        def build(q):
            flat = grid_ref[:, s0 : s0 + SC + 2].reshape(6 * (SC + 2), 8, 128)
            turned = [flat, pltpu.roll(flat, 7, 1), pltpu.roll(flat, 6, 1)]
            shift = (16 - 32 * q) % 128
            parts = []
            for d, lanes in enumerate((shift, shift + 64, shift)):
                moved = pltpu.roll(turned[d], lanes % 128, 2).reshape(6, SC + 2, 8, 128)
                own = moved[:, 1:-1]
                at = 64 * (d % 2)
                if q == 0:
                    own = jnp.where((lane >= at) & (lane < at + 16), moved[:, :-2], own)
                if q == 3:
                    own = jnp.where((lane >= at + 48) & (lane < at + 64), moved[:, 2:], own)
                parts.append(own)
            first = jnp.where(lane < 64, parts[0], parts[1])
            pieces.append(jnp.concatenate([first, parts[2]], axis=-1))

        def gather():
            patch = jnp.stack(pieces, axis=2).reshape(6, SC * 4 * 8, 256).astype(BF16)
            patch = jnp.concatenate([patch[k : k + 4] for k in range(3)], axis=-1)
            pieces.append(patch.reshape(4 * SC * 32, 768))

        def expand(n):
            out = jnp.dot(pieces[-1], band_ref[:, 256 * n : 256 * (n + 1)], preferred_element_type=F32)
            hidden.append(out.reshape(4, SC * 32, 256))

        def norm(t):
            tiles = []
            for pp in range(2):
                h = []
                for k in range(3):
                    n = 3 * pp + k
                    lanes = slice(128 * (n % 2), 128 * (n % 2) + 128)
                    h.append(hidden[n // 2][t][:, lanes] + b_in[:, 128 * k : 128 * (k + 1)])
                mean = jnp.sum(h[0] * h[0] + h[1] * h[1] + h[2] * h[2], axis=-1, keepdims=True) * (1.0 / 384)
                factor = lax.rsqrt(mean + 1e-6)
                tiles.append([silu_of_half(h[k] * factor * g_in[:, 128 * k : 128 * (k + 1)]) for k in range(3)])
            merged = []
            for k in range(3):
                v = jnp.stack([tiles[pp][k].reshape(SC * 4, 8, 128) for pp in range(2)], axis=1)
                if t < 2:
                    v = jnp.where(frame > 0, v, 0.0)
                merged.append(v.reshape(SC * 64, 128).astype(BF16))
            feats.append(merged)

        def align():
            rows = [jnp.concatenate([v for k in range(3) for v in feats[t + k]], axis=-1) for t in range(2)]
            hist.append(jnp.concatenate(rows, axis=0))

        def double(n):
            acc = jnp.dot(hist[0], wtime_ref[:, 256 * n : 256 * (n + 1)], preferred_element_type=F32)
            acc = (acc + b_time[:, 256 * n : 256 * (n + 1)]).reshape(2, SC * 8, 8, 256)
            for i in range(2):
                j, k = (2 * n + i) // 3, (2 * n + i) % 3
                for t in range(2):
                    lanes = acc[t, :, :, 128 * i : 128 * (i + 1)]
                    dbl_ref[k, 8 * s0 + 1 : 8 * (s0 + SC) + 1, pl.ds(2 * j + t, 8, stride=4), :] = lanes

        return (
            [functools.partial(build, q) for q in range(4)] + [gather] + [functools.partial(expand, n) for n in range(3)],
            [functools.partial(norm, t) for t in range(4)],
            [align] + [functools.partial(double, n) for n in range(3)],
        )

    chunks = [chunk(s0) for s0 in range(0, 16, SC)]
    for turn in range(len(chunks) + 2):
        if turn in waits:
            waits[turn].wait()
        weave(*(chunks[turn - n][n] for n in range(3) if 0 <= turn - n < len(chunks)))

    @pl.when(top)
    def _():
        dbl_ref[:, :, 0:4, :] = jnp.zeros((3, dbl_ref.shape[1], 4, 128), F32)

    @pl.when(bottom)
    def _():
        dbl_ref[:, :, 20:24, :] = jnp.zeros((3, dbl_ref.shape[1], 4, 128), F32)


class Columns:
    def __init__(self, step, sub, dbl_ref, wl_ref, bl_ref, gl_ref, wf_ref, bf_ref, out_ref, rows_ref, sec_ref):
        row = lax.axis_index("rows")
        self.top, self.bottom = row == 0, row == lax.axis_size("rows") - 1
        self.width = dbl_ref.shape[1] - 2
        self.x0, self.sub, self.count = step * XB + sub, sub, SUB + 1
        self.low = lax.broadcasted_iota(jnp.int32, (1, 1, 128), 2) < 64
        self.lane = lax.broadcasted_iota(jnp.int32, (1, 1, 128), 2)
        self.half = lax.broadcasted_iota(jnp.int32, (1, 8, 1), 1) < 4
        self.dbl_ref, self.wl_ref, self.bl_ref, self.gl_ref = dbl_ref, wl_ref, bl_ref, gl_ref
        self.wf_ref, self.bf_ref, self.out_ref, self.rows_ref = wf_ref, bf_ref, out_ref, rows_ref
        self.sec_ref = sec_ref.at[sub // SUB]
        self.acc, self.results, self.s_m, self.s_p, self.s_e = {}, {}, [], [], []

    def load(self):
        patch = []
        for ty in range(2):
            tiles = [self.dbl_ref[k, pl.ds(self.x0, self.count + 1), 4 * ty : 4 * ty + 24, :] for k in range(3)]
            patch += [
                v[tx : tx + self.count].reshape(self.count * 24, 128).astype(BF16) for tx in range(2) for v in tiles
            ]
        self.patch = jnp.concatenate(patch, axis=-1)

    def lift_steps(self):
        def part(n):
            w = self.wl_ref[:, 256 * n : 256 * (n + 1)]
            acc = jnp.dot(self.patch, w, preferred_element_type=F32)
            self.acc[n] = acc.reshape(self.count, 24, 256)

        return [self.load] + [functools.partial(part, n) for n in range(3)]

    def keep(self, n, lo, hi, v):
        px, k = n // 3, n % 3
        first_rows = lax.broadcasted_iota(jnp.int32, (1, 8, 1), 1) < 4
        above, below = jnp.logical_and(first_rows, self.top), jnp.logical_and(first_rows, self.bottom)
        for g in range(3):
            part = v[:, 8 * g : 8 * (g + 1)]
            if g == 0 and k < 2:
                part = jnp.where(above if k == 0 else jnp.logical_and(above, self.low), 0.0, part)
            if g == 2 and k > 0:
                part = jnp.where(below if k == 2 else jnp.logical_and(below, jnp.logical_not(self.low)), 0.0, part)
            rows = slice(16 + 8 * g, 24 + 8 * g)
            if px == 0 and lo == 0:
                self.sec_ref[n, 0:1, rows, :] = jnp.where(self.x0 == 0, 0.0, part[0:1])
                self.sec_ref[n, 1:hi, rows, :] = part[1:]
            elif px == 1 and hi == self.count:
                self.sec_ref[n, lo : hi - 1, rows, :] = part[:-1]
                self.sec_ref[n, hi - 1 : hi, rows, :] = jnp.where(self.x0 == self.width - SUB, 0.0, part[-1:])
            else:
                self.sec_ref[n, lo:hi, rows, :] = part

    def norm_steps(self):
        def part(lo, hi, px):
            tiles = []
            for k in range(3):
                n = 3 * px + k
                lanes = slice(128 * (n % 2), 128 * (n % 2) + 128)
                tiles.append(self.acc[n // 2][lo:hi, :, lanes] + self.bl_ref[:, 128 * n : 128 * (n + 1)])
            sq = [v * v for v in tiles]
            s0 = jnp.sum(sq[0] + jnp.where(self.low, sq[1], 0.0), axis=-1, keepdims=True)
            s1 = jnp.sum(sq[2] + jnp.where(self.low, 0.0, sq[1]), axis=-1, keepdims=True)
            f0 = lax.rsqrt(s0 * (1.0 / 192) + 1e-6)
            f1 = lax.rsqrt(s1 * (1.0 / 192) + 1e-6)
            for k, f in enumerate((f0, jnp.where(self.low, f0, f1), f1)):
                n = 3 * px + k
                v = silu_of_half(tiles[k] * f * self.gl_ref[:, 128 * n : 128 * (n + 1)])
                self.keep(n, lo, hi, v)

        cuts = [self.count * c // NCH for c in range(NCH + 1)]
        return [functools.partial(part, lo, hi, px) for px in range(2) for lo, hi in zip(cuts, cuts[1:])]

    def window(self, k, first):
        out = []
        for h in range(2):
            lo = self.sec_ref[k, :, pl.ds(16 + 4 * first + 2 * h, 8, stride=4), :]
            hi = self.sec_ref[k, :, pl.ds(4 * first + 2 * h + 1, 8, stride=4), :]
            out.append(jnp.where(self.half, lo, hi))
        return jnp.concatenate(out, axis=1).astype(BF16)

    def final_steps(self):
        def windows():
            self.s_m = [self.window(k, 0) for k in range(6)]
            self.s_p = [self.window(k, 1) for k in range(6)]
            for px in range(2):
                mixed = jnp.where(self.low, self.s_p[3 * px + 1], self.s_m[3 * px + 1])
                self.s_e += [self.s_p[3 * px], mixed, self.s_m[3 * px + 2]]

        def mul(a, source, kind, lo, even):
            tiles = getattr(self, source)
            if even:
                tiles = [v[1:] for v in tiles[:3]] + [v[:-1] for v in tiles[3:]]
            lhs = jnp.concatenate(tiles, axis=-1).reshape(-1, 768)
            w = self.wf_ref[kind, :, lo : lo + 256]
            self.results[a, even] = jnp.dot(lhs, w, preferred_element_type=F32).reshape(-1, 16, 256)

        plan = ((1, "s_e", 1, 0), (2, "s_e", 1, 256), (0, "s_m", 3, 256), (3, "s_p", 3, 0))
        steps = [windows]
        for a, source, kind, lo in plan:
            steps += [
                functools.partial(mul, a, source, kind, lo, False),
                functools.partial(mul, a, source, kind - 1, lo, True),
                functools.partial(self.place, a),
            ]
        return steps

    def place(self, a):
        o, e = self.results[a, False], self.results[a, True]
        t0 = jnp.where(self.lane < 96, o[:-1, :, 128:], e[..., :128])
        t1 = e[..., 128:]
        t2 = jnp.where(self.lane < 32, e[..., :128], o[1:, :, :128])
        for k, t in enumerate((t0, t1, t2)):
            t = t + self.bf_ref[:, 128 * k : 128 * (k + 1)]
            for u in range(SUB):
                self.rows_ref[3 * (self.sub + u) + k, pl.ds(a, 16, stride=4), :] = t[u]

    def store_steps(self):
        def part(j, t):
            base = 16 * (2 * j + t)
            for n in range(3 * self.sub, 3 * (self.sub + SUB)):
                rows = self.rows_ref[n, base : base + 16, :]
                self.out_ref[2 * t + j, :, 128 * n : 128 * (n + 1)] = rows.astype(BF16)

        return [functools.partial(part, j, t) for j in range(2) for t in range(2)]


def back(step, *refs):
    parts = [Columns(step, sub, *refs) for sub in range(0, XB, SUB)]
    last = len(parts) - 1
    for turn in range(len(parts) + 3):
        lists = []
        if turn <= last:
            lists.append(parts[turn].lift_steps())
        if 0 <= turn - 1 <= last:
            lists.append(parts[turn - 1].norm_steps())
        if 0 <= turn - 2 <= last:
            lists.append(parts[turn - 2].final_steps())
        if 0 <= turn - 3 <= last:
            lists.append(parts[turn - 3].store_steps())
        weave(*lists)


def spread(half):
    wide, narrow = half[:, :128], half[:, 128:]
    return jnp.concatenate([wide, narrow, narrow, wide] * 2, axis=-1)


def decode_kernel(count, *refs):
    sources, out_ref, copies = refs[:count], refs[count], refs[count + 1 : 2 * count + 1]
    grid_ref, dbl_ref, rows_ref, sec_ref, bl_ref, gl_ref, bf_ref, load_sem = refs[2 * count + 1 :]
    blocks, (bin_ref, gin_ref, btime_ref, blift_ref, glift_ref, bfinal_ref) = copies[:3], copies[3:9]
    band_ref, wtime_ref, wl_ref, wf_ref = copies[9:]
    step = pl.program_id(0)

    @pl.when(step == 0)
    def _():
        loads = [pltpu.make_async_copy(src, dst, load_sem.at[n]) for n, (src, dst) in enumerate(zip(sources, copies))]
        for copy in loads:
            copy.start()
        for copy in loads[:9]:
            copy.wait()
        bl_ref[...] = spread(blift_ref[...].reshape(1, -1))
        gl_ref[...] = 0.5 * spread(glift_ref[...].reshape(1, -1))
        bf_ref[...] = jnp.concatenate([bfinal_ref[...].reshape(1, -1)] * 4, axis=-1)
        waits = {0: loads[9], 2: loads[10]}
        front(blocks, band_ref, bin_ref, gin_ref, wtime_ref, btime_ref, grid_ref, dbl_ref, waits)
        loads[11].wait()
        loads[12].wait()

    back(step, dbl_ref, wl_ref, bl_ref, gl_ref, wf_ref, bf_ref, out_ref, rows_ref, sec_ref)


def decode(above, own, below, band, wl, wf, b_in, gain_in, w_time, b_time, b_lift, gain_lift, b_final):
    width = 128
    hbm = pl.BlockSpec(memory_space=pltpu.HBM)
    w_time = w_time.reshape(-1, w_time.shape[-1])
    args = (above, own, below, b_in, gain_in, b_time, b_lift, gain_lift, b_final, band, w_time, wl, wf)
    return pl.pallas_call(
        functools.partial(decode_kernel, len(args)),
        grid=(width // XB,),
        in_specs=[hbm] * len(args),
        out_specs=pl.BlockSpec((4, 16, XB * 384), lambda i: (0, 0, i)),
        out_shape=jax.ShapeDtypeStruct((4, 16, width * 384), BF16),
        scratch_shapes=[pltpu.VMEM(v.shape, v.dtype) for v in args]
        + [
            pltpu.VMEM((6, 18, 8, 128), F32),
            pltpu.VMEM((3, width + 2, 32, 128), F32),
            pltpu.VMEM((XB * 3, 64, 128), F32),
            pltpu.VMEM((XB // SUB, 6, SUB + 1, 56, 128), F32),
            pltpu.VMEM((1, 768), F32),
            pltpu.VMEM((1, 768), F32),
            pltpu.VMEM((1, 384), F32),
            pltpu.SemaphoreType.DMA((len(args),)),
        ],
        compiler_params=pltpu.CompilerParams(vmem_limit_bytes=VMEM_LIMIT),
        name="decode",
    )(*args)


def far_first(count):
    return sorted(range(1, count), key=lambda k: -min(k, count - k))


def exchange_kernel(
    rows, frames,
    lat_hbm, slot_hbm, win_hbm, wlift_hbm, wfinal_hbm,
    above, own, below, band_hbm, lift_hbm, final_hbm,
    lat_ref, slot_ref, send1, recv1, send2, recv2, block, win_ref, wlift_ref, wfinal_ref, band_ref, lift_ref, final_ref,
    load_sem, store_sem, send_sem1, recv_sem1, send_sem2, recv_sem2, send_sem3, recv_sem3,
):
    r, f = lax.axis_index("rows"), lax.axis_index("frames")
    loads = [
        pltpu.make_async_copy(src, dst, load_sem.at[n])
        for n, (src, dst) in enumerate(
            (
                (win_hbm, win_ref), (wlift_hbm, wlift_ref), (wfinal_hbm, wfinal_ref),
                (lat_hbm, lat_ref), (slot_hbm, slot_ref),
            )
        )
    ]
    loads[4].start()
    loads[3].start()

    def at(dr, df):
        return {"rows": lax.rem(r + dr + rows, rows), "frames": lax.rem(f + df + frames, frames)}

    near = [(dr, df) for df in (2, 1, 0) for dr in (1, -1, 0) if (dr, df) != (0, 0)]
    far = [(dr, df) for dr, df in near if dr != 0 and df != 0]
    barrier = pltpu.get_barrier_semaphore()
    sources = [(-dr, -df) for dr, df in far] + [(0, k) for k in far_first(frames)] + [(k, 0) for k in far_first(rows)]
    for dr, df in sources:
        pl.semaphore_signal(barrier, inc=1, device_id=at(dr, df), device_id_type=pl.DeviceIdType.MESH)

    for copy in loads[:3]:
        copy.start()
    loads[4].wait()
    loads[3].wait()

    slots, width = lat_ref.shape
    across = jnp.broadcast_to(slot_ref[...].reshape(1, slots), (slots, slots))
    down = across.T
    index = lax.broadcasted_iota(jnp.int32, (slots, slots), 0)
    lane = lax.broadcasted_iota(jnp.int32, (slots, slots), 1)
    twin = jnp.logical_and(across // slots == down // slots, index < lane)
    rank = jnp.sum(jnp.where(twin, 1, 0), axis=0, keepdims=True)
    target = 2 * (across[:1] // slots) + rank
    total = 2 * rows * frames
    place = lax.broadcasted_iota(jnp.int32, (total, slots), 0) == target
    tags = (down % slots + 1).astype(F32).astype(BF16)
    tagged = jnp.concatenate([lat_ref[...], tags], axis=-1)
    packed = jnp.dot(jnp.where(place, 1.0, 0.0).astype(BF16), tagged, preferred_element_type=F32)
    send1[...] = packed.astype(BF16).reshape(send1.shape)
    recv1[r] = send1[r]
    pl.semaphore_wait(barrier, len(sources))

    def remote(src, dst, send, recv, dr, df):
        return pltpu.make_async_remote_copy(
            src_ref=src, dst_ref=dst, send_sem=send, recv_sem=recv,
            device_id=at(dr, df), device_id_type=pl.DeviceIdType.MESH,
        )

    first = []
    for k in far_first(rows):
        peer, source = lax.rem(r + k, rows), lax.rem(r - k + rows, rows)
        out = remote(send1.at[peer], recv1.at[r], send_sem1.at[k], recv_sem1.at[k], k, 0)
        out.start()
        first.append((out, remote(send1.at[peer], recv1.at[source], send_sem1.at[k], recv_sem1.at[k], k, 0)))
    loads[0].wait()
    make_band(win_ref, band_ref)
    loads[1].wait()
    make_lift(wlift_ref, lift_ref, 0, 0)
    for out, arrival in first:
        arrival.wait_recv()

    o = lax.broadcasted_iota(jnp.int32, (total, total), 0)
    i = lax.broadcasted_iota(jnp.int32, (total, total), 1)
    group = 2 * rows
    regroup = i == ((o // 2) % rows) * (2 * frames) + (o // group) * 2 + o % 2
    moved = jnp.dot(
        jnp.where(regroup, 1.0, 0.0).astype(BF16), recv1[...].reshape(total, 2 * width), preferred_element_type=F32
    )
    send2[...] = moved.astype(BF16).reshape(send2.shape)
    recv2[f] = send2[f]
    second = []
    for k in far_first(frames):
        peer, source = lax.rem(f + k, frames), lax.rem(f - k + frames, frames)
        out = remote(send2.at[peer], recv2.at[f], send_sem2.at[k], recv_sem2.at[k], 0, k)
        out.start()
        second.append((out, remote(send2.at[peer], recv2.at[source], send_sem2.at[k], recv_sem2.at[k], 0, k)))
    make_lift(wlift_ref, lift_ref, 0, 1)
    make_lift(wlift_ref, lift_ref, 1, 0)
    for out, arrival in second:
        arrival.wait_recv()

    arrived = recv2[...].reshape(total, 2 * width)
    want = lax.broadcasted_iota(jnp.int32, (total, slots), 1).astype(F32) + 1.0
    land = jnp.where(arrived[:, width:].astype(F32) == want, 1.0, 0.0).astype(BF16)
    canvas = lax.dot_general(land, arrived[:, :width], (((0,), (0,)), ((), ())), preferred_element_type=F32)
    block[...] = canvas.astype(BF16).reshape(2, 64, width)
    third = []
    for n, (dr, df) in enumerate(near):
        src, region = {
            0: (block, own),
            1: (block.at[:, pl.ds(32, 32)], above),
            -1: (block.at[:, pl.ds(0, 32)], below),
        }[dr]
        out = remote(src, region.at[2 - df], send_sem3.at[n], recv_sem3.at[n], dr, df)
        out.start()
        third.append(out)
    keep = pltpu.make_async_copy(block, own.at[2], load_sem.at[5])
    keep.start()
    make_lift(wlift_ref, lift_ref, 1, 1)
    loads[2].wait()
    for part in range(3):
        make_final(wfinal_ref, final_ref, part)
    stores = [
        pltpu.make_async_copy(src, dst, store_sem.at[n])
        for n, (src, dst) in enumerate(((band_ref, band_hbm), (lift_ref, lift_hbm), (final_ref, final_hbm)))
    ]
    for copy in stores:
        copy.start()
    for out in third:
        out.wait_recv()
    keep.wait()
    for out, _ in first + second:
        out.wait_send()
    for out in third:
        out.wait_send()
    for copy in stores:
        copy.wait()


def exchange(latents, tile_slot, w_in, w_lift, w_final):
    rows, frames = lax.axis_size("rows"), lax.axis_size("frames")
    width = latents.shape[1]
    hbm = pl.BlockSpec(memory_space=pltpu.HBM)
    weights = (w_in, w_lift.swapaxes(2, 3), w_final)
    made = [(768, 768), (1536, 768), (4, 768, 512)]
    blocks = [(3, 2, 32, width), (3, 2, 64, width), (3, 2, 32, width)]
    dma = pltpu.SemaphoreType.DMA
    return pl.pallas_call(
        functools.partial(exchange_kernel, rows, frames),
        in_specs=[hbm] * 5,
        out_specs=[hbm] * 6,
        out_shape=[jax.ShapeDtypeStruct(shape, BF16) for shape in blocks + made],
        scratch_shapes=[
            pltpu.VMEM(latents.shape, BF16),
            pltpu.VMEM(tile_slot.shape, jnp.int32),
            pltpu.VMEM((rows, 2 * frames, 2 * width), BF16),
            pltpu.VMEM((rows, 2 * frames, 2 * width), BF16),
            pltpu.VMEM((frames, 2 * rows, 2 * width), BF16),
            pltpu.VMEM((frames, 2 * rows, 2 * width), BF16),
            pltpu.VMEM((2, 64, width), BF16),
        ]
        + [pltpu.VMEM(w.shape, BF16) for w in weights]
        + [pltpu.VMEM(shape, BF16) for shape in made]
        + [dma((6,)), dma((3,)), dma((rows,)), dma((rows,)), dma((frames,)), dma((frames,)), dma((8,)), dma((8,))],
        compiler_params=pltpu.CompilerParams(
            collective_id=0, has_side_effects=True, vmem_limit_bytes=VMEM_LIMIT
        ),
        name="exchange",
    )(latents, tile_slot, *weights)


def shards(
    latents, tile_slot, w_in, b_in, gain_in, w_time, b_time, w_lift, b_lift, gain_lift, w_final, b_final
):
    above, own, below, band, wl, wf = exchange(latents, tile_slot, w_in, w_lift, w_final)
    return decode(above, own, below, band, wl, wf, b_in, gain_in, w_time, b_time, b_lift, gain_lift, b_final)


def solution(mesh):
    in_specs = (P(("rows", "frames"), None), P(("rows", "frames"))) + (P(),) * 10
    out_specs = P("frames", "rows", None)
    return jax.shard_map(shards, mesh=mesh, in_specs=in_specs, out_specs=out_specs, check_vma=False)
```
